256 devices in a mesh: seq: 32 (over x, y, core), head: 8 (over z).
Axes of the slice: x: 4, y: 4, z: 8, core: 2. Of those that a mesh axis runs over, the one named last changes fastest.
Arguments:
- queries: bfloat16 [16384, 2048], P('seq', 'head'), may hold values from -6 to 6
- keys: bfloat16 [16384, 2048], P('seq', 'head'), may hold values from -6 to 6
- values: bfloat16 [16384, 2048], P('seq', 'head'), may hold values from -6 to 6
- attn_out: bfloat16 [16384, 2048], P('seq', 'head'), may hold values from -4 to 4
- out_grad: bfloat16 [16384, 4096], P(('seq', 'head')), may hold values from -48 to 48
- out_weight: bfloat16 [2048, 4096], P('head'), may hold values from -0.125 to 0.125
- log_norm: bfloat16 [16384, 16], P('seq', 'head'), may hold values from 0 to 13
- block_sizes: int32 [512], replicated, may hold values from 1 to 31, as said below
Outputs:
- query_grad: bfloat16 [16384, 2048], P('seq', 'head')
- key_grad: bfloat16 [16384, 2048], P('seq', 'head')
- value_grad: bfloat16 [16384, 2048], P('seq', 'head')
The draws below stay inside these ranges and needn't reach their ends.
Inputs may be any that keep to these rules, and one draw needn't show every extreme that they name: `block_sizes`: blocks come in aligned pairs whose sizes add to 32; one block has exactly 31 tokens.
All inputs are finite; a program needn't handle non-finite values.
Results may differ from the reference program's by a relative error of at most 0.018.
Values may be sent and summed in bfloat16 or wider, within the bound.
A program may use at most 128 MiB of HBM per device.

```python
import math
import jax
import jax.numpy as jnp
from jax import lax

D = 4096
HD = 128
HEADS = 16
TOK_DEV = 512
BLK_MEAN = 16
SEQ = 16384
HALF = 8192
NBLK = 512


def pair_sizes(key):
    pairs = NBLK // 2
    offsets = jax.random.randint(jax.random.fold_in(key, 11), (pairs,), -(BLK_MEAN - 1), BLK_MEAN)
    chosen = jax.random.randint(jax.random.fold_in(key, 12), (), 0, pairs)
    offsets = jnp.where(jnp.arange(pairs) == chosen, BLK_MEAN - 1, offsets)
    return jnp.stack([BLK_MEAN + offsets, BLK_MEAN - offsets], axis=1).reshape(NBLK).astype(jnp.int32)


def column_shift(key):
    bits = jax.random.randint(jax.random.fold_in(key, 21), (HEADS * HD,), 0, 2)
    level = math.sqrt(0.5 * math.log(HALF / (2.0 * BLK_MEAN)) / math.sqrt(HD))
    return (2 * bits - 1).astype(jnp.float32) * level


def draw_block_sizes(key, part):
    sizes = pair_sizes(key)
    return sizes


def draw_queries(key, part):
    shift = column_shift(key)
    key = jax.random.fold_in(key, 5)
    entries = jax.random.normal(key, (SEQ, HEADS * HD), jnp.float32)
    noisy = (jnp.arange(SEQ, dtype=jnp.int32) < HALF)[:, None]
    moved = entries - jnp.where(noisy, shift[None, :], 0.0)
    return jnp.clip(moved, -6.0, 6.0).astype(jnp.bfloat16)


def draw_keys(key, part):
    shift = column_shift(key)
    key = jax.random.fold_in(key, 9)
    entries = jax.random.normal(key, (SEQ, HEADS * HD), jnp.float32)
    noisy = (jnp.arange(SEQ, dtype=jnp.int32) < HALF)[:, None]
    moved = entries + jnp.where(noisy, 0.0, shift[None, :])
    return jnp.clip(moved, -6.0, 6.0).astype(jnp.bfloat16)


def draw_log_norm(key, part):
    key = jax.random.fold_in(key, 7)
    clean_level = math.log(HALF) + 0.5
    noisy_level = 0.5 * math.log(HALF * BLK_MEAN) + 0.5
    noisy = jnp.arange(SEQ, dtype=jnp.int32) < HALF
    base = jnp.where(noisy, noisy_level, clean_level).astype(jnp.float32)
    jitter = jax.random.uniform(key, (SEQ, HEADS), jnp.float32, -0.25, 0.25)
    return (base[:, None] + jitter).astype(jnp.bfloat16)


def level_of(key, shape, pieces, smallest, top_value):
    level = 1.0
    for dim, shards_of in pieces:
        steps = jax.random.uniform(jax.random.fold_in(jax.random.fold_in(key, 6), dim), (shards_of,), jnp.float32, smallest / len(pieces), top_value / len(pieces))
        level = level * jnp.repeat(jnp.exp(steps), shape[dim] // shards_of).reshape((-1,) + (1,) * (len(shape) - 1 - dim))
    return level


def bell_draw(key, dims, scale, most, cuts=(), kind=jnp.bfloat16):
    factor_of = level_of(key, dims, cuts, -0.22, 0.18) if cuts else 1.0
    result = jax.random.normal(key, dims, jnp.float32) * scale * factor_of
    return jnp.minimum(jnp.maximum(result, -most), most).astype(kind)


def setup_inputs(seed: int = 0) -> dict:
    splits = jax.random.split(jax.random.key(seed), 9)
    return {
        "queries": draw_queries(jax.random.fold_in(splits[8], 71), 0),
        "keys": draw_keys(jax.random.fold_in(splits[8], 71), 0),
        "values": bell_draw(splits[2], (SEQ, HEADS * HD), 1.0, 6.0, ((0, 32), (1, 8))),
        "attn_out": bell_draw(splits[3], (SEQ, HEADS * HD), 0.3, 4.0, ((0, 32), (1, 8))),
        "out_grad": bell_draw(splits[4], (SEQ, D), 8.0, 48.0, ((0, 256),)),
        "out_weight": bell_draw(splits[5], (HEADS * HD, D), (HEADS * HD) ** -0.5, 0.125, ((0, 8),)),
        "log_norm": draw_log_norm(jax.random.fold_in(splits[8], 71), 0),
        "block_sizes": draw_block_sizes(jax.random.fold_in(splits[8], 71), 0),
    }


def block_index(within, ends):
    return jnp.sum((within[:, None] >= ends[None, :]).astype(jnp.int32), axis=1)


def allowed_pairs(query_block, query_noisy, key_block, key_noisy):
    qb = query_block[:, None]
    kb = key_block[None, :]
    qn = query_noisy[:, None]
    kn = key_noisy[None, :]
    noisy_rows = qn & ((kn & (kb == qb)) | (jnp.logical_not(kn) & (kb < qb)))
    clean_rows = jnp.logical_not(qn) & jnp.logical_not(kn) & (kb <= qb)
    return noisy_rows | clean_rows


def reference(queries, keys, values, attn_out, out_grad, out_weight, log_norm, block_sizes):
    ends = jnp.cumsum(block_sizes).astype(jnp.int32)
    position = jnp.arange(SEQ, dtype=jnp.int32)
    noisy = position < HALF
    block = block_index(position % HALF, ends)
    head_grad = jnp.dot(out_grad, out_weight.T, preferred_element_type=jnp.float32).astype(jnp.bfloat16)
    delta = (head_grad.astype(jnp.float32) * attn_out.astype(jnp.float32)).reshape(SEQ, HEADS, HD).sum(-1).astype(jnp.bfloat16)
    scale = HD ** -0.5
    count = SEQ // TOK_DEV

    def one_head(head):
        first = (head * HD).astype(jnp.int32)
        query_head = lax.dynamic_slice_in_dim(queries, first, HD, 1)
        key_head = lax.dynamic_slice_in_dim(keys, first, HD, 1)
        value_head = lax.dynamic_slice_in_dim(values, first, HD, 1)
        grad_head = lax.dynamic_slice_in_dim(head_grad, first, HD, 1)
        norm_head = lax.dynamic_slice_in_dim(log_norm, head, 1, 1)[:, 0].astype(jnp.float32)
        delta_head = lax.dynamic_slice_in_dim(delta, head, 1, 1)[:, 0].astype(jnp.float32)

        def step(sums, index):
            start = (index * TOK_DEV).astype(jnp.int32)
            query_rows = lax.dynamic_slice_in_dim(query_head, start, TOK_DEV, 0)
            grad_rows = lax.dynamic_slice_in_dim(grad_head, start, TOK_DEV, 0)
            norm_rows = lax.dynamic_slice_in_dim(norm_head, start, TOK_DEV, 0)
            delta_rows = lax.dynamic_slice_in_dim(delta_head, start, TOK_DEV, 0)
            mask = allowed_pairs(lax.dynamic_slice_in_dim(block, start, TOK_DEV, 0), lax.dynamic_slice_in_dim(noisy, start, TOK_DEV, 0), block, noisy)
            score = jnp.dot(query_rows, key_head.T, preferred_element_type=jnp.float32)
            probs = jnp.where(mask, jnp.exp(score * scale - norm_rows[:, None]), 0.0)
            probs_half = probs.astype(jnp.bfloat16)
            value_add = jnp.dot(probs_half.T, grad_rows, preferred_element_type=jnp.float32)
            prob_grad = jnp.dot(grad_rows, value_head.T, preferred_element_type=jnp.float32)
            score_grad = (probs * (prob_grad - delta_rows[:, None]) * scale).astype(jnp.bfloat16)
            query_part = jnp.dot(score_grad, key_head, preferred_element_type=jnp.float32).astype(jnp.bfloat16)
            key_add = jnp.dot(score_grad.T, query_rows, preferred_element_type=jnp.float32)
            return (sums[0] + key_add, sums[1] + value_add), query_part

        zero_sum = jnp.zeros((SEQ, HD), jnp.float32)
        sums, query_parts = lax.scan(step, (zero_sum, zero_sum), jnp.arange(count, dtype=jnp.int32))
        return query_parts.reshape(SEQ, HD), sums[0].astype(jnp.bfloat16), sums[1].astype(jnp.bfloat16)

    query_all, key_all, value_all = lax.map(one_head, jnp.arange(HEADS, dtype=jnp.int32))

    def join(stacked):
        return jnp.transpose(stacked, (1, 0, 2)).reshape(SEQ, HEADS * HD)

    return join(query_all), join(key_all), join(value_all)
```

```python
import functools
import math

import jax
import jax.numpy as jnp
from jax import lax
from jax.experimental import pallas as pl
from jax.experimental.pallas import tpu as pltpu
from jax.sharding import PartitionSpec as P

HD = 128
UNIT = 32
ROWS = 512
STRIPE = 128
TASK_Q = 4096
TASK_K = 2048
PEERS = 32
SHARDS = 16
SCALE = HD ** -0.5
MESH = pl.DeviceIdType.MESH
F32 = jnp.float32
BF16 = jnp.bfloat16
CONTRACT_LAST = (((1,), (1,)), ((), ()))
CONTRACT_FIRST = (((0,), (0,)), ((), ()))


def where_am_i():
    seq = lax.axis_index("seq")
    x, y, core = seq // 8, (seq // 2) % 4, seq % 2
    return seq, x, y, core


def own_rows(seq):
    x, y, core = seq // 8, (seq // 2) % 4, seq % 2
    slot = x % 2
    group = y + slot * (3 - 2 * y)
    return group, slot * 2048 + (x // 2) * 1024 + core * ROWS


def multiple(value, of):
    return pl.multiple_of(value, of)


def push(here, there, device, me, send_sem, recv_sem):
    seq, head = device

    @pl.when(seq == me)
    def _():
        pltpu.make_async_copy(here, there, recv_sem).start()

    @pl.when(seq != me)
    def _():
        pltpu.make_async_remote_copy(
            src_ref=here, dst_ref=there, send_sem=send_sem, recv_sem=recv_sem,
            device_id=(seq, head), device_id_type=MESH,
        ).start()


def wait_bytes(ref, sem):
    pltpu.make_async_copy(ref, ref, sem).wait()


def greet_plane(barrier, me, head):
    def greet(step, carry):
        pl.semaphore_signal(
            barrier, inc=1, device_id=(lax.rem(me + step, PEERS), head), device_id_type=MESH
        )
        return carry

    lax.fori_loop(1, PEERS, greet, 0)


def spread_kernel(
    q_ref, k_ref, v_ref, o_ref, g_ref, w_ref, n_ref,
    qg, dg, kg, vg, dl,
    from_left, from_right,
    ring_send, ring_recv, q_send, k_send, v_send, d_send, q_recv, k_recv, v_recv, d_recv,
):
    me, x, y, core = where_am_i()
    head = lax.axis_index("head")
    right, left = lax.rem(head + 1, 8), lax.rem(head + 7, 8)
    group, row0 = own_rows(me)
    place = me % SHARDS
    clean = me >= SHARDS

    barrier = pltpu.get_barrier_semaphore()
    greet_plane(barrier, me, head)
    for neighbour in (left, right):
        pl.semaphore_signal(barrier, inc=1, device_id=(me, neighbour), device_id_type=MESH)
    pl.semaphore_wait(barrier, PEERS + 1)

    def ring(direction, index):
        landed = (from_left, from_right)[direction]
        if index < 2:
            unit = index if direction == 0 else 1 - index
            source = g_ref.at[pl.ds(unit * UNIT, UNIT)]
        else:
            source = landed.at[index - 2]
        return pltpu.make_async_remote_copy(
            src_ref=source,
            dst_ref=landed.at[index],
            send_sem=ring_send.at[direction, index],
            recv_sem=ring_recv.at[direction, index],
            device_id=(me, (right, left)[direction]),
            device_id_type=MESH,
        )

    for index in range(2):
        for direction in range(2):
            ring(direction, index).start()

    def task_of(index):
        return (index // 2 * 4 + group) * 2 + index % 2

    def send_queries(step, carry):
        index = lax.rem(me + step, 8)
        column = multiple(index % 2 * HD, HD)
        push(
            q_ref.at[:, pl.ds(column, HD)],
            qg.at[pl.ds(multiple(row0, ROWS), ROWS)],
            (task_of(index), head), me, q_send.at[index], q_recv,
        )
        return carry

    lax.fori_loop(0, 8, send_queries, 0)

    @pl.when(clean)
    def _():
        def send_keys(step, carry):
            device = lax.rem(me + step, PEERS)
            row = multiple(device // 8 * STRIPE, STRIPE)
            column = multiple(device % 2 * HD, HD)
            target = pl.ds(multiple(place * STRIPE, STRIPE), STRIPE)
            for source, landed, send, recv in ((k_ref, kg, k_send, k_recv), (v_ref, vg, v_send, v_recv)):
                push(
                    source.at[pl.ds(row, STRIPE), pl.ds(column, HD)],
                    landed.at[target],
                    (device, head), me, send.at[device], recv,
                )
            return carry

        lax.fori_loop(0, PEERS, send_keys, 0)

    lane = lax.broadcasted_iota(jnp.int32, (UNIT, HD), 1)

    def produce(unit_ref, owner, unit):
        start = multiple(owner * 64 + unit * UNIT, UNIT)
        rows = pl.ds(start, UNIT)
        grad = lax.dot_general(
            unit_ref[...], w_ref[...], CONTRACT_LAST, preferred_element_type=F32
        ).astype(BF16)
        for h in range(2):
            columns = slice(h * HD, (h + 1) * HD)
            part = grad[:, columns]
            delta = jnp.sum(
                part.astype(F32) * o_ref[rows, columns].astype(F32), axis=1, keepdims=True
            ).astype(BF16)
            norm = n_ref[rows, :].astype(F32)[:, h:h + 1] * (1.0 / SCALE)
            high = norm.astype(BF16)
            rest = norm - high.astype(F32)
            middle = rest.astype(BF16)
            low = (rest - middle.astype(F32)).astype(BF16)
            extra = jnp.where(lane == 0, high.astype(F32), 0.0)
            extra = jnp.where(lane == 1, middle.astype(F32), extra)
            extra = jnp.where(lane == 2, low.astype(F32), extra)
            extra = jnp.where(lane == 3, delta.astype(F32), extra)
            dl[rows, h * 256:h * 256 + HD] = part
            dl[rows, h * 256 + HD:(h + 1) * 256] = extra.astype(BF16)

        def send(step, carry):
            index = lax.rem(me + step, 8)
            column = multiple(index % 2 * 256, 256)
            push(
                dl.at[rows, pl.ds(column, 256)],
                dg.at[pl.ds(multiple(row0 + start, UNIT), UNIT)],
                (task_of(index), head), me, d_send.at[index], d_recv,
            )
            return carry

        lax.fori_loop(0, 8, send, 0)

    for unit in range(2):
        produce(g_ref.at[pl.ds(unit * UNIT, UNIT)], head, unit)
    for index in range(7):
        for direction in range(2):
            ring(direction, index).wait_recv()
            if index < 5:
                ring(direction, index + 2).start()
        away = index // 2 + 1
        produce(from_left.at[index], lax.rem(head + 8 - away, 8), index % 2)
        produce(from_right.at[index], lax.rem(head + away, 8), 1 - index % 2)

    wait_bytes(dg, d_recv)
    wait_bytes(qg, q_recv)
    wait_bytes(kg, k_recv)
    wait_bytes(vg, v_recv)
    for index in range(7):
        for direction in range(2):
            ring(direction, index).wait_send()

    def settle(index, carry):
        @pl.when(task_of(index) != me)
        def _():
            wait_bytes(q_ref.at[:, pl.ds(0, HD)], q_send.at[index])
            wait_bytes(dl.at[:, pl.ds(0, 256)], d_send.at[index])
        return carry

    lax.fori_loop(0, 8, settle, 0)

    @pl.when(clean)
    def _():
        def settle_keys(step, carry):
            device = lax.rem(me + step, PEERS)
            wait_bytes(k_ref.at[pl.ds(0, STRIPE), pl.ds(0, HD)], k_send.at[device])
            wait_bytes(v_ref.at[pl.ds(0, STRIPE), pl.ds(0, HD)], v_send.at[device])
            return carry

        lax.fori_loop(1, PEERS, settle_keys, 0)


def dot(a, b, dims):
    return lax.dot_general(a, b, dims, preferred_element_type=F32)


def pick(shape, first, last):
    lane = lax.broadcasted_iota(jnp.int32, shape, 1)
    return jnp.where((lane >= first) & (lane <= last), -1.0, 0.0).astype(BF16)


def tile(q, d, k, v, mask):
    rows = k.shape[0]
    keys = jnp.concatenate([k, pick((rows, HD), 0, 2)], axis=1)
    values = jnp.concatenate([v, pick((rows, HD), 3, 3)], axis=1)
    score = dot(jnp.concatenate([q, d[:, HD:]], axis=1), keys, CONTRACT_LAST)
    probs = jnp.exp2(score * (SCALE * math.log2(math.e)))
    if mask is not None:
        probs = jnp.where(mask, probs, 0.0)
    grad = (probs * dot(d, values, CONTRACT_LAST)).astype(BF16)
    dq = dot(grad, k, (((1,), (0,)), ((), ())))
    dk = dot(grad, q, CONTRACT_FIRST)
    dv = dot(probs.astype(BF16), d[:, :HD], CONTRACT_FIRST)
    return dq, dk, dv


TILE_Q = 512


def attend_kernel(
    sizes, qg, dg, kg, vg, q_ref, k_ref, v_ref, dl,
    dq_out, dk_out, dv_out, dq_own, dk_own, dv_own,
    dq_sum, dk_sum, dv_sum, row_block, own_block,
):
    me, x, y, core = where_am_i()
    group, stripe = y, x
    place = me % SHARDS
    dq_sum[...] = jnp.zeros_like(dq_sum)
    dk_sum[...] = jnp.zeros_like(dk_sum)
    dv_sum[...] = jnp.zeros_like(dv_sum)

    def coarse_of(slot):
        return group + slot * (7 - 2 * group)

    in_group = lax.broadcasted_iota(jnp.int32, (32, HD), 0)

    def number_rows(index, carry):
        pair = coarse_of(index // 32) * 32 + index % 32
        row_block[pl.ds(multiple(index * 32, 32), 32), :] = 2 * pair + jnp.where(
            in_group >= sizes[2 * pair], 1, 0
        )
        return carry

    lax.fori_loop(0, 64, number_rows, 0)

    lane = lax.broadcasted_iota(jnp.int32, (1, HD), 1)

    def key_blocks(coarse, half):
        pair = (coarse * 1024 + half * ROWS + stripe * STRIPE) // 32
        part = lane // 32
        size = jnp.where(
            part < 2,
            jnp.where(part == 0, sizes[2 * pair], sizes[2 * pair + 2]),
            jnp.where(part == 2, sizes[2 * pair + 4], sizes[2 * pair + 6]),
        )
        return 2 * (pair + part) + jnp.where(lane % 32 >= size, 1, 0)

    def step(slot, pair, blocks):
        keys = pl.ds(multiple(pair * 256, 256), 256)

        def inner(index, carry):
            rows = pl.ds(multiple(slot * 2048 + index * TILE_Q, TILE_Q), TILE_Q)
            mask = None
            if blocks is not None:
                per = 1024 // TILE_Q
                start = multiple(slot * 1024 + index % per * TILE_Q, TILE_Q)
                own = row_block[pl.ds(start, TILE_Q), :] + index // per
                mask = jnp.concatenate([own, own], axis=1) > blocks
            dq, dk, dv = tile(qg[rows, :], dg[rows, :], kg[keys, :], vg[keys, :], mask)
            dq_sum[rows, :] += dq
            dk_sum[keys, :] += dk
            dv_sum[keys, :] += dv
            return carry

        lax.fori_loop(0, 2048 // TILE_Q, inner, 0)

    for slot in range(2):
        coarse = coarse_of(slot)

        def full(pair, carry):
            step(slot, pair, None)
            return carry

        lax.fori_loop(0, coarse, full, 0)
        step(slot, coarse, jnp.concatenate([key_blocks(coarse, 0), key_blocks(coarse, 1)], axis=1))

    dq_out[...] = (dq_sum[...] * SCALE).astype(BF16)
    dk_out[...] = (dk_sum[...] * SCALE).astype(BF16)
    dv_out[...] = dv_sum[...].astype(BF16)

    @pl.when(me < SHARDS)
    def _():
        def number_own(index, carry):
            pair = place * 16 + index
            own_block[pl.ds(multiple(index * 32, 32), 32), :] = 2 * pair + jnp.where(
                in_group >= sizes[2 * pair], 1, 0
            )
            return carry

        lax.fori_loop(0, 16, number_own, 0)
        for part in range(4):
            rows = slice(part * STRIPE, (part + 1) * STRIPE)
            block = own_block[rows, :].astype(F32)
            mask = block == block.T
            for h in range(2):
                columns = slice(h * HD, (h + 1) * HD)
                dq, dk, dv = tile(
                    q_ref[rows, columns], dl[rows, h * 256:(h + 1) * 256],
                    k_ref[rows, columns], v_ref[rows, columns], mask,
                )
                dq_own[rows, columns] = (dq * SCALE).astype(BF16)
                dk_own[rows, columns] = (dk * SCALE).astype(BF16)
                dv_own[rows, columns] = dv.astype(BF16)


def collect_kernel(
    dq, dk, dv, dq_own, dk_own, dv_own,
    dq_out, dk_out, dv_out,
    rq, rk, rv,
    q_send, k_send, v_send, q_recv, k_recv, v_recv,
):
    me, x, y, core = where_am_i()
    head = lax.axis_index("head")
    clean = me >= SHARDS
    barrier = pltpu.get_barrier_semaphore()
    greet_plane(barrier, me, head)
    pl.semaphore_wait(barrier, PEERS - 1)
    columns = pl.ds(multiple(core * HD, HD), HD)

    def query_owner(index):
        slot, kind, half = index // 4, index // 2 % 2, index % 2
        coarse = y + slot * (7 - 2 * y)
        return kind * SHARDS + 2 * coarse + half

    def send_queries(step, carry):
        index = lax.rem(me + step, 8)
        push(
            dq.at[pl.ds(multiple(index * ROWS, ROWS), ROWS)],
            rq.at[x, :, columns],
            (query_owner(index), head), me, q_send.at[index], q_recv,
        )
        return carry

    def send_keys(step, carry):
        index = lax.rem(me + step, SHARDS)
        rows = pl.ds(multiple(index * STRIPE, STRIPE), STRIPE)
        target = pl.ds(multiple(x * STRIPE, STRIPE), STRIPE)
        for source, landed, send, recv in ((dk, rk, k_send, k_recv), (dv, rv, v_send, v_recv)):
            push(
                source.at[rows],
                landed.at[y, target, columns],
                (SHARDS + index, head), me, send.at[index], recv,
            )
        return carry

    lax.fori_loop(0, SHARDS, send_keys, 0)
    lax.fori_loop(0, 8, send_queries, 0)

    wait_bytes(rq, q_recv)

    @pl.when(clean)
    def _():
        dq_out[...] = (
            (rq[0].astype(F32) + rq[1].astype(F32)) + (rq[2].astype(F32) + rq[3].astype(F32))
        ).astype(BF16)
        wait_bytes(rk, k_recv)
        wait_bytes(rv, v_recv)
        for landed, out in ((rk, dk_out), (rv, dv_out)):
            out[...] = (
                (landed[0].astype(F32) + landed[1].astype(F32))
                + (landed[2].astype(F32) + landed[3].astype(F32))
            ).astype(BF16)

    @pl.when(me < SHARDS)
    def _():
        dq_out[...] = (
            (rq[0].astype(F32) + rq[1].astype(F32)) + (rq[2].astype(F32) + rq[3].astype(F32))
            + dq_own[...].astype(F32)
        ).astype(BF16)
        dk_out[...] = dk_own[...]
        dv_out[...] = dv_own[...]

    def settle_queries(index, carry):
        @pl.when(query_owner(index) != me)
        def _():
            wait_bytes(dq.at[pl.ds(0, ROWS)], q_send.at[index])
        return carry

    lax.fori_loop(0, 8, settle_queries, 0)

    def settle_keys(index, carry):
        @pl.when(SHARDS + index != me)
        def _():
            wait_bytes(dk.at[pl.ds(0, STRIPE)], k_send.at[index])
            wait_bytes(dv.at[pl.ds(0, STRIPE)], v_send.at[index])
        return carry

    lax.fori_loop(0, SHARDS, settle_keys, 0)


ANY = pl.BlockSpec(memory_space=pl.ANY)
VMEM = pl.BlockSpec(memory_space=pltpu.VMEM)
SMEM = pl.BlockSpec(memory_space=pltpu.SMEM)
DMA = pltpu.SemaphoreType.DMA
LIMIT = 56 * 1024 * 1024


def half_array(*shape):
    return jax.ShapeDtypeStruct(shape, BF16)


def spread(queries, keys, values, attn_out, out_grad, out_weight, log_norm):
    return pl.pallas_call(
        spread_kernel,
        name="spread",
        out_shape=(
            half_array(TASK_Q, HD), half_array(TASK_Q, 256), half_array(TASK_K, HD),
            half_array(TASK_K, HD), half_array(ROWS, 512),
        ),
        in_specs=[ANY, ANY, ANY, VMEM, VMEM, VMEM, VMEM],
        out_specs=(ANY, ANY, ANY, ANY, VMEM),
        scratch_shapes=[
            pltpu.VMEM((7, UNIT, 4096), BF16),
            pltpu.VMEM((7, UNIT, 4096), BF16),
            DMA((2, 7)), DMA((2, 7)), DMA((8,)), DMA((PEERS,)), DMA((PEERS,)), DMA((8,)),
            DMA, DMA, DMA, DMA,
        ],
        compiler_params=pltpu.CompilerParams(
            collective_id=0, has_side_effects=True, vmem_limit_bytes=LIMIT
        ),
    )(queries, keys, values, attn_out, out_grad, out_weight, log_norm)


def attend(block_sizes, spread_out, queries, keys, values):
    qg, dg, kg, vg, dl = spread_out
    return pl.pallas_call(
        attend_kernel,
        name="attend",
        out_shape=(
            half_array(TASK_Q, HD), half_array(TASK_K, HD), half_array(TASK_K, HD),
            half_array(ROWS, 256), half_array(ROWS, 256), half_array(ROWS, 256),
        ),
        in_specs=[SMEM] + [VMEM] * 8,
        out_specs=(VMEM,) * 6,
        scratch_shapes=[
            pltpu.VMEM((TASK_Q, HD), F32),
            pltpu.VMEM((TASK_K, HD), F32),
            pltpu.VMEM((TASK_K, HD), F32),
            pltpu.VMEM((2048, HD), jnp.int32),
            pltpu.VMEM((ROWS, HD), jnp.int32),
        ],
        compiler_params=pltpu.CompilerParams(vmem_limit_bytes=LIMIT),
    )(block_sizes, qg, dg, kg, vg, queries, keys, values, dl)


def collect(parts):
    return pl.pallas_call(
        collect_kernel,
        name="collect",
        out_shape=(half_array(ROWS, 256),) * 3,
        in_specs=[VMEM] * 6,
        out_specs=(VMEM,) * 3,
        scratch_shapes=[
            pltpu.VMEM((4, ROWS, 256), BF16),
            pltpu.VMEM((4, ROWS, 256), BF16),
            pltpu.VMEM((4, ROWS, 256), BF16),
            DMA((8,)), DMA((SHARDS,)), DMA((SHARDS,)),
            DMA, DMA, DMA,
        ],
        compiler_params=pltpu.CompilerParams(
            collective_id=1, has_side_effects=True, vmem_limit_bytes=LIMIT
        ),
    )(*parts)


def shards(queries, keys, values, attn_out, out_grad, out_weight, log_norm, block_sizes):
    moved = spread(queries, keys, values, attn_out, out_grad, out_weight, log_norm)
    parts = attend(block_sizes, moved, queries, keys, values)
    return collect(parts)


def solution(mesh):
    in_specs = (
        P("seq", "head"),
        P("seq", "head"),
        P("seq", "head"),
        P("seq", "head"),
        P(("seq", "head"), None),
        P("head", None),
        P("seq", "head"),
        P(),
    )
    out_specs = (P("seq", "head"), P("seq", "head"), P("seq", "head"))
    return jax.shard_map(shards, mesh=mesh, in_specs=in_specs, out_specs=out_specs, check_vma=False)
```

```python
import functools
import math

import jax
import jax.numpy as jnp
from jax import lax
from jax.experimental import pallas as pl
from jax.experimental.pallas import tpu as pltpu
from jax.sharding import PartitionSpec as P

HD = 128
UNIT = 32
ROWS = 512
STRIPE = 128
TASK_K = 2048
PEERS = 32
SHARDS = 16
SCALE = HD ** -0.5
MESH = pl.DeviceIdType.MESH
F32 = jnp.float32
BF16 = jnp.bfloat16
CONTRACT = (((1,), (0,)), ((), ()))
CONTRACT_LAST = (((1,), (1,)), ((), ()))
CONTRACT_FIRST = (((0,), (0,)), ((), ()))


def where_am_i():
    seq = lax.axis_index("seq")
    return seq, seq // 8, (seq // 2) % 4, seq % 2


def multiple(value, of):
    return pl.multiple_of(value, of)


def push(here, there, device, me, send_sem, recv_sem):
    seq, head = device

    @pl.when(seq == me)
    def _():
        pltpu.make_async_copy(here, there, recv_sem).start()

    @pl.when(seq != me)
    def _():
        pltpu.make_async_remote_copy(
            src_ref=here, dst_ref=there, send_sem=send_sem, recv_sem=recv_sem,
            device_id=(seq, head), device_id_type=MESH,
        ).start()


def wait_bytes(ref, sem):
    pltpu.make_async_copy(ref, ref, sem).wait()


def dot(a, b, dims):
    return lax.dot_general(a, b, dims, preferred_element_type=F32)


def tile(q, d, keys, values, mask):
    score = dot(jnp.concatenate([q, d[:, HD:]], axis=1), keys, CONTRACT_LAST)
    probs = jnp.exp2(score * (SCALE * math.log2(math.e)))
    if mask is not None:
        probs = jnp.where(mask, probs, 0.0)
    grad = (probs * dot(d, values, CONTRACT_LAST)).astype(BF16)
    dq = dot(grad, keys[:, :HD], CONTRACT)
    dk = dot(grad, q, CONTRACT_FIRST)
    dv = dot(probs.astype(BF16), d[:, :HD], CONTRACT_FIRST)
    return dq, dk, dv


def pick(rows, first, last):
    lane = lax.broadcasted_iota(jnp.int32, (rows, HD), 1)
    return jnp.where((lane >= first) & (lane <= last), -1.0, 0.0).astype(BF16)


def layer_kernel(
    sizes, q_ref, k_ref, v_ref, o_ref, g_ref, w_ref, n_ref,
    dq_out, dk_out, dv_out,
    landed, qg, dg, kg, vg, dl,
    dq_sum, dk_sum, dv_sum, row_block, key_block, own_block, dq_own,
    dq_part, to_sibling, from_sibling, key_part, rq, rk,
    ring_send, ring_recv, q_send, k_send, v_send, d_send, q_recv, k_recv, v_recv, d_recv,
    dq_send, dq_recv, sibling_send, sibling_recv, part_send, part_recv,
):
    me, x, y, core = where_am_i()
    head = lax.axis_index("head")
    right, left = lax.rem(head + 1, 8), lax.rem(head + 7, 8)
    place = me % SHARDS
    clean = me >= SHARDS
    own_slot = x % 2
    own_group = y + own_slot * (3 - 2 * y)
    own_row = (x // 2) * 128 + core * 64
    group = y // 2 * 2 + core
    which = y % 2
    sibling = me + 1 - 2 * core

    barrier = pltpu.get_barrier_semaphore()

    def greet(step, carry):
        pl.semaphore_signal(
            barrier, inc=1, device_id=(lax.rem(me + step, PEERS), head), device_id_type=MESH
        )
        return carry

    lax.fori_loop(1, PEERS, greet, 0)
    for neighbour in (left, right):
        pl.semaphore_signal(barrier, inc=1, device_id=(me, neighbour), device_id_type=MESH)
    pl.semaphore_wait(barrier, PEERS + 1)

    def ring(direction, index, source):
        return pltpu.make_async_remote_copy(
            src_ref=source,
            dst_ref=landed.at[index, direction],
            send_sem=ring_send.at[direction, index],
            recv_sem=ring_recv.at[direction, index],
            device_id=(me, (right, left)[direction]),
            device_id_type=MESH,
        )

    for index in range(2):
        for direction in range(2):
            unit = index if direction == 0 else 1 - index
            ring(direction, index, g_ref.at[pl.ds(unit * UNIT, UNIT)]).start()

    def task_of(index):
        stripe, part = index // 2, index % 2
        return (stripe * 4 + own_group // 2 * 2 + part) * 2 + own_group % 2

    def send_queries(step, carry):
        index = lax.rem(me + step, 8)
        column = multiple(index % 2 * HD, HD)
        push(
            q_ref.at[:, :, pl.ds(column, HD)],
            qg.at[own_slot, :, pl.ds(multiple(own_row, 64), 64)],
            (task_of(index), head), me, q_send.at[index], q_recv,
        )
        return carry

    lax.fori_loop(0, 8, send_queries, 0)

    @pl.when(clean)
    def _():
        def send_keys(step, carry):
            device = lax.rem(me + step, PEERS)
            row = multiple(device // 8 * STRIPE, STRIPE)
            column = multiple(device // 2 % 2 * HD, HD)
            target = pl.ds(multiple(place * STRIPE, STRIPE), STRIPE)
            for source, there, send, recv in ((k_ref, kg, k_send, k_recv), (v_ref, vg, v_send, v_recv)):
                push(
                    source.at[pl.ds(row, STRIPE), pl.ds(column, HD)],
                    there.at[target, pl.ds(0, HD)],
                    (device, head), me, send.at[device], recv,
                )
            return carry

        lax.fori_loop(0, PEERS, send_keys, 0)

    lane = lax.broadcasted_iota(jnp.int32, (UNIT, HD), 1)

    def produce(grad, start):
        rows = pl.ds(multiple(start, UNIT), UNIT)
        norms = n_ref[rows, :].astype(F32) * (1.0 / SCALE)
        for h in range(2):
            columns = slice(h * HD, (h + 1) * HD)
            part = grad[:, columns]
            delta = jnp.sum(
                part.astype(F32) * o_ref[rows, columns].astype(F32), axis=1, keepdims=True
            ).astype(BF16).astype(F32)
            norm = norms[:, h:h + 1]
            high = norm.astype(BF16).astype(F32)
            rest = norm - high
            middle = rest.astype(BF16).astype(F32)
            low = rest - middle
            extra = jnp.where(lane == 0, high, 0.0)
            extra = jnp.where(lane == 1, middle, extra)
            extra = jnp.where(lane == 2, low, extra)
            extra = jnp.where(lane == 3, delta, extra)
            dl[rows, h * 256:h * 256 + HD] = part
            dl[rows, h * 256 + HD:(h + 1) * 256] = extra.astype(BF16)

    def project(rows):
        return dot(rows, w_ref[...], CONTRACT_LAST).astype(BF16)

    def send_grads(chunk):
        def send(step, carry):
            index = lax.rem(me + step, 8)
            column = multiple(index % 2 * 256, 256)
            push(
                dl.at[pl.ds(multiple(chunk * 64, 64), 64), pl.ds(column, 256)],
                dg.at[own_slot, chunk, pl.ds(multiple(own_row, 64), 64)],
                (task_of(index), head), me, d_send.at[index], d_recv.at[chunk],
            )
            return carry

        lax.fori_loop(0, 8, send, 0)

    grad = project(g_ref[...])
    for unit in range(2):
        produce(grad[unit * UNIT:(unit + 1) * UNIT], head * 64 + unit * UNIT)
    send_grads(head)

    kg[:, HD:] = pick(TASK_K, 0, 2)
    vg[:, HD:] = pick(TASK_K, 3, 3)
    dk_sum[...] = jnp.zeros_like(dk_sum)
    dv_sum[...] = jnp.zeros_like(dv_sum)
    in_group = lax.broadcasted_iota(jnp.int32, (32, HD), 0)

    def coarse_of(slot):
        return group + slot * (7 - 2 * group)

    def number_rows(index, carry):
        slot, chunk, half, pair = index // 32, index // 4 % 8, index // 2 % 2, index % 2
        pair = coarse_of(slot) * 32 + half * 16 + chunk * 2 + pair
        block = 2 * pair + jnp.where(in_group >= sizes[2 * pair], 1, 0)
        row = half * 64 + index % 2 * 32
        row_block[slot, chunk, pl.ds(multiple(row, 32), 32), :] = block
        row_block[slot, chunk, pl.ds(multiple(128 + row, 32), 32), :] = block + 1
        return carry

    lax.fori_loop(0, 64, number_rows, 0)
    row_lane = lax.broadcasted_iota(jnp.int32, (1, HD), 1)

    def number_keys(index, carry):
        blocks = []
        for half in range(2):
            pair = (index * 1024 + half * ROWS + x * STRIPE) // 32
            part = row_lane // 32
            size = jnp.where(
                part < 2,
                jnp.where(part == 0, sizes[2 * pair], sizes[2 * pair + 2]),
                jnp.where(part == 2, sizes[2 * pair + 4], sizes[2 * pair + 6]),
            )
            blocks.append(2 * (pair + part) + jnp.where(row_lane % 32 >= size, 1, 0))
        key_block[index] = jnp.concatenate(blocks, axis=1)
        return carry

    lax.fori_loop(0, 8, number_keys, 0)

    def query_owner(index):
        slot, kind, half = index // 4, index // 2 % 2, index % 2
        return kind * SHARDS + 2 * coarse_of(slot) + half

    def attend(turn, carry):
        chunk = lax.rem(head + 8 + (turn + 1) // 2 * (1 - 2 * (turn % 2)), 8)

        @pl.when(turn == 0)
        def _():
            wait_bytes(qg, q_recv)
            wait_bytes(kg.at[:, pl.ds(0, HD)], k_recv)
            wait_bytes(vg.at[:, pl.ds(0, HD)], v_recv)

        wait_bytes(dg.at[:, chunk], d_recv.at[chunk])
        dq_sum[...] = jnp.zeros_like(dq_sum)
        later = None
        for number in range(9):
            slot = 1 if number >= 4 else (number - group + 3) // 4
            pair = number - slot * (group + 1)
            keys = pl.ds(multiple(pair * 256, 256), 256)
            mask = None
            if number < 4 or number == 8:
                own = row_block[slot, chunk]
                mask = jnp.concatenate([own, own], axis=1) > key_block[pair]
            dq, dk, dv = tile(qg[slot, chunk], dg[slot, chunk], kg[keys, :], vg[keys, :], mask)
            dk_sum[keys, :] += dk
            dv_sum[keys, :] += dv
            if number < 4:
                dq_sum[slot] += dq
            else:
                later = dq if later is None else later + dq
        first = (dq_sum[0] * SCALE).astype(BF16)
        second = ((dq_sum[1] + later) * SCALE).astype(BF16)
        for index in range(8):
            part = (first, second)[index // 4]
            dq_part[chunk, index] = part[index % 4 * 64:(index % 4 + 1) * 64]

        def send(step, inner):
            index = lax.rem(me + step, 8)
            push(
                dq_part.at[chunk, index],
                rq.at[x, chunk, :, pl.ds(multiple(which * HD, HD), HD)],
                (query_owner(index), head), me, dq_send.at[index], dq_recv,
            )
            return inner

        lax.fori_loop(0, 8, send, 0)
        return carry

    def attended(step):
        return step - (step + 7) // 8 + step // 6 + step // 7

    def step(index, carry):
        for direction in range(2):
            ring(direction, index, landed.at[index, direction]).wait_recv()

            @pl.when(index < 5)
            def _():
                ring(direction, lax.rem(index + 2, 7), landed.at[index, direction]).start()

        away = index // 2 + 1
        chunks = (lax.rem(head + 8 - away, 8), lax.rem(head + away, 8))
        units = (index % 2, 1 - index % 2)
        grad = project(landed[index].reshape(2 * UNIT, 4096))
        for direction in range(2):
            produce(
                grad[direction * UNIT:(direction + 1) * UNIT],
                chunks[direction] * 64 + units[direction] * UNIT,
            )

        @pl.when(index % 2 == 1)
        def _():
            send_grads(chunks[0])

        @pl.when((index % 2 == 1) | (index == 6))
        def _():
            send_grads(chunks[1])

        lax.fori_loop(attended(index), attended(index + 1), attend, 0)
        return carry

    lax.fori_loop(0, 7, step, 0)

    def narrow(index, carry):
        there = pl.ds(multiple(index * 256 + (1 - core) * STRIPE, STRIPE), STRIPE)
        to_sibling[0, index] = (dk_sum[there, :] * SCALE).astype(BF16)
        to_sibling[1, index] = dv_sum[there, :].astype(BF16)
        return carry

    lax.fori_loop(0, 8, narrow, 0)
    across = pltpu.make_async_remote_copy(
        src_ref=to_sibling, dst_ref=from_sibling, send_sem=sibling_send, recv_sem=sibling_recv,
        device_id=(sibling, head), device_id_type=MESH,
    )
    across.start()
    across.wait_recv()

    def pass_on(step, carry):
        index = lax.rem(me // 2 + step, 8)
        here = pl.ds(multiple(index * 256 + core * STRIPE, STRIPE), STRIPE)
        key_part[index, 0] = (
            dk_sum[here, :] * SCALE + from_sibling[0, index].astype(F32)
        ).astype(BF16)
        key_part[index, 1] = (dv_sum[here, :] + from_sibling[1, index].astype(F32)).astype(BF16)
        push(
            key_part.at[index],
            rk.at[y // 2, :, pl.ds(multiple(x * STRIPE, STRIPE), STRIPE), pl.ds(multiple(which * HD, HD), HD)],
            (SHARDS + 2 * index + core, head), me, part_send.at[index], part_recv,
        )
        return carry

    lax.fori_loop(0, 8, pass_on, 0)

    @pl.when(me < SHARDS)
    def _():
        def number_own(index, carry):
            pair = place * 16 + index
            own_block[pl.ds(multiple(index * 32, 32), 32), :] = 2 * pair + jnp.where(
                in_group >= sizes[2 * pair], 1, 0
            )
            return carry

        lax.fori_loop(0, 16, number_own, 0)
        for part in range(4):
            rows = slice(part * STRIPE, (part + 1) * STRIPE)
            block = own_block[rows, :].astype(F32)
            mask = block == block.T
            for h in range(2):
                columns = slice(h * HD, (h + 1) * HD)
                dq, dk, dv = tile(
                    q_ref[2 * part:2 * part + 2, :, columns].reshape(STRIPE, HD),
                    dl[rows, h * 256:(h + 1) * 256],
                    jnp.concatenate([k_ref[rows, columns], pick(STRIPE, 0, 2)], axis=1),
                    jnp.concatenate([v_ref[rows, columns], pick(STRIPE, 3, 3)], axis=1),
                    mask,
                )
                dq_own[rows, columns] = dq * SCALE
                dk_out[rows, columns] = (dk * SCALE).astype(BF16)
                dv_out[rows, columns] = dv.astype(BF16)

    wait_bytes(rq, dq_recv)

    def summed_queries():
        parts = [rq[stripe].reshape(ROWS, 256).astype(F32) for stripe in range(4)]
        return (parts[0] + parts[1]) + (parts[2] + parts[3])

    @pl.when(me < SHARDS)
    def _():
        dq_out[...] = (summed_queries() + dq_own[...]).astype(BF16)

    @pl.when(clean)
    def _():
        dq_out[...] = summed_queries().astype(BF16)
        wait_bytes(rk, part_recv)
        dk_out[...] = (rk[0, 0].astype(F32) + rk[1, 0].astype(F32)).astype(BF16)
        dv_out[...] = (rk[0, 1].astype(F32) + rk[1, 1].astype(F32)).astype(BF16)

    for index in range(7):
        for direction in range(2):
            ring(direction, index, landed.at[index, direction]).wait_send()
    across.wait_send()

    def settle(index, carry):
        @pl.when(task_of(index) != me)
        def _():
            wait_bytes(q_ref.at[:, :, pl.ds(0, HD)], q_send.at[index])
            wait_bytes(dl.at[:, pl.ds(0, 256)], d_send.at[index])

        @pl.when(query_owner(index) != me)
        def _():
            wait_bytes(dq_part.at[:, index], dq_send.at[index])

        @pl.when(SHARDS + 2 * index + core != me)
        def _():
            wait_bytes(key_part.at[index], part_send.at[index])
        return carry

    lax.fori_loop(0, 8, settle, 0)

    @pl.when(clean)
    def _():
        def settle_keys(step, carry):
            device = lax.rem(me + step, PEERS)
            wait_bytes(k_ref.at[pl.ds(0, STRIPE), pl.ds(0, HD)], k_send.at[device])
            wait_bytes(v_ref.at[pl.ds(0, STRIPE), pl.ds(0, HD)], v_send.at[device])
            return carry

        lax.fori_loop(1, PEERS, settle_keys, 0)


VMEM = pl.BlockSpec(memory_space=pltpu.VMEM)
SMEM = pl.BlockSpec(memory_space=pltpu.SMEM)
DMA = pltpu.SemaphoreType.DMA
LIMIT = 56 * 1024 * 1024


def shards(queries, keys, values, attn_out, out_grad, out_weight, log_norm, block_sizes):
    return pl.pallas_call(
        layer_kernel,
        name="layer",
        out_shape=(jax.ShapeDtypeStruct((ROWS, 256), BF16),) * 3,
        in_specs=[SMEM] + [VMEM] * 7,
        out_specs=(VMEM,) * 3,
        scratch_shapes=[
            pltpu.VMEM((7, 2, UNIT, 4096), BF16),
            pltpu.VMEM((2, 8, 256, HD), BF16),
            pltpu.VMEM((2, 8, 256, 256), BF16),
            pltpu.VMEM((TASK_K, 256), BF16),
            pltpu.VMEM((TASK_K, 256), BF16),
            pltpu.VMEM((ROWS, 512), BF16),
            pltpu.VMEM((2, 256, HD), F32),
            pltpu.VMEM((TASK_K, HD), F32),
            pltpu.VMEM((TASK_K, HD), F32),
            pltpu.VMEM((2, 8, 256, HD), jnp.int32),
            pltpu.VMEM((8, 1, 256), jnp.int32),
            pltpu.VMEM((ROWS, HD), jnp.int32),
            pltpu.VMEM((ROWS, 256), F32),
            pltpu.VMEM((8, 8, 64, HD), BF16),
            pltpu.VMEM((2, 8, STRIPE, HD), BF16),
            pltpu.VMEM((2, 8, STRIPE, HD), BF16),
            pltpu.VMEM((8, 2, STRIPE, HD), BF16),
            pltpu.VMEM((4, 8, 64, 256), BF16),
            pltpu.VMEM((2, 2, ROWS, 256), BF16),
            DMA((2, 7)), DMA((2, 7)), DMA((8,)), DMA((PEERS,)), DMA((PEERS,)), DMA((8,)),
            DMA, DMA, DMA, DMA((8,)),
            DMA((8,)), DMA, DMA, DMA, DMA((8,)), DMA,
        ],
        compiler_params=pltpu.CompilerParams(
            collective_id=0, has_side_effects=True, vmem_limit_bytes=LIMIT
        ),
    )(
        block_sizes, queries.reshape(8, 64, 256), keys, values, attn_out, out_grad, out_weight,
        log_norm,
    )


def solution(mesh):
    in_specs = (
        P("seq", "head"),
        P("seq", "head"),
        P("seq", "head"),
        P("seq", "head"),
        P(("seq", "head"), None),
        P("head", None),
        P("seq", "head"),
        P(),
    )
    out_specs = (P("seq", "head"), P("seq", "head"), P("seq", "head"))
    return jax.shard_map(shards, mesh=mesh, in_specs=in_specs, out_specs=out_specs, check_vma=False)
```

```python
import functools
import math

import jax
import jax.numpy as jnp
from jax import lax
from jax.experimental import pallas as pl
from jax.experimental.pallas import tpu as pltpu
from jax.sharding import PartitionSpec as P

HD = 128
UNIT = 32
SIDE = 16
ROWS = 512
STRIPE = 128
TASK_K = 2048
PEERS = 32
SHARDS = 16
CHIPS = 16
SCALE = HD ** -0.5
MESH = pl.DeviceIdType.MESH
F32 = jnp.float32
BF16 = jnp.bfloat16
CONTRACT = (((1,), (0,)), ((), ()))
CONTRACT_LAST = (((1,), (1,)), ((), ()))
CONTRACT_FIRST = (((0,), (0,)), ((), ()))


def where_am_i():
    seq = lax.axis_index("seq")
    return seq, seq // 8, (seq // 2) % 4, seq % 2


def multiple(value, of):
    return pl.multiple_of(value, of)


def push(here, there, device, me, send_sem, recv_sem):
    seq, head = device

    @pl.when(seq == me)
    def _():
        pltpu.make_async_copy(here, there, recv_sem).start()

    @pl.when(seq != me)
    def _():
        pltpu.make_async_remote_copy(
            src_ref=here, dst_ref=there, send_sem=send_sem, recv_sem=recv_sem,
            device_id=(seq, head), device_id_type=MESH,
        ).start()


def wait_bytes(ref, sem):
    pltpu.make_async_copy(ref, ref, sem).wait()


def dot(a, b, dims):
    return lax.dot_general(a, b, dims, preferred_element_type=F32)


def tile(q, d, extra, keys, values, mask):
    score = dot(jnp.concatenate([q, extra], axis=1), keys, CONTRACT_LAST)
    probs = jnp.exp2(score * (SCALE * math.log2(math.e)))
    if mask is not None:
        probs = jnp.where(mask, probs, 0.0)
    grad = (probs * dot(jnp.concatenate([d, extra], axis=1), values, CONTRACT_LAST)).astype(BF16)
    dq = dot(grad, keys[:, :HD], CONTRACT)
    dk = dot(grad, q, CONTRACT_FIRST)
    dv = dot(probs.astype(BF16), d, CONTRACT_FIRST)
    return dq, dk, dv


def pick(rows, first, last):
    lane = lax.broadcasted_iota(jnp.int32, (rows, HD), 1)
    part = lane % SIDE
    return jnp.where((lane < 4 * SIDE) & (part >= first) & (part <= last), -1.0, 0.0).astype(BF16)


def side(pieces):
    stacked = jnp.concatenate([piece.astype(F32) for piece in pieces], axis=0)
    filler = jnp.zeros((HD - stacked.shape[0], HD), F32)
    turned = jnp.concatenate([stacked, filler], axis=0).T[:64]
    lane = lax.broadcasted_iota(jnp.int32, (64, HD), 1)
    return jnp.concatenate(
        [jnp.where(lane // SIDE == number, turned, 0.0) for number in range(len(pieces))], axis=0
    ).astype(BF16)


def layer_kernel(
    sizes, q_ref, k_ref, v_ref, o_ref, g_ref, w_ref, n_ref,
    dq_out, dk_out, dv_out,
    landed, qg, dg, kg, vg, dl, norms, extras,
    dq_sum, dk_sum, dv_sum, row_block, key_block, own_block, dq_own,
    dq_part, to_sibling, from_sibling, key_part, rq, rk,
    ring_send, ring_recv, q_send, k_send, v_send, d_send, q_recv, k_recv, v_recv, d_recv,
    dq_send, dq_recv, sibling_send, sibling_recv, part_send, part_recv, relay_send,
):
    me, x, y, core = where_am_i()
    head = lax.axis_index("head")
    right, left = lax.rem(head + 1, 8), lax.rem(head + 7, 8)
    place = me % SHARDS
    clean = me >= SHARDS
    own_slot = x % 2
    own_group = y + own_slot * (3 - 2 * y)
    own_piece = (x // 2) * 2 + core
    group = core * 2 + y % 2
    which = y // 2
    sibling = me + 1 - 2 * core

    barrier = pltpu.get_barrier_semaphore()

    def greet(step, carry):
        pl.semaphore_signal(
            barrier, inc=1, device_id=(lax.rem(me + step, PEERS), head), device_id_type=MESH
        )
        return carry

    lax.fori_loop(1, PEERS, greet, 0)
    for neighbour in (left, right):
        pl.semaphore_signal(barrier, inc=1, device_id=(me, neighbour), device_id_type=MESH)
    pl.semaphore_wait(barrier, PEERS + 1)

    def ring(direction, index, source):
        return pltpu.make_async_remote_copy(
            src_ref=source,
            dst_ref=landed.at[index, direction],
            send_sem=ring_send.at[direction, index],
            recv_sem=ring_recv.at[direction, index],
            device_id=(me, (right, left)[direction]),
            device_id_type=MESH,
        )

    for index in range(2):
        for direction in range(2):
            unit = index if direction == 0 else 1 - index
            ring(direction, index, g_ref.at[pl.ds(unit * UNIT, UNIT)]).start()

    def task_of(index):
        stripe, part = index // 2, index % 2
        return (stripe * 4 + 2 * part + own_group % 2) * 2 + own_group // 2

    def send_queries(step, carry):
        index = lax.rem(me + step, 8)
        column = multiple(index % 2 * HD, HD)
        push(
            q_ref.at[:, :, pl.ds(column, HD)],
            qg.at[own_slot, :, pl.ds(multiple(own_piece * 64, 64), 64)],
            (task_of(index), head), me, q_send.at[index], q_recv,
        )
        return carry

    lax.fori_loop(0, 8, send_queries, 0)

    @pl.when(clean)
    def _():
        def send_keys(step, carry):
            chip = lax.rem(me // 2 + step, CHIPS)
            row = multiple(chip // 4 * STRIPE, STRIPE)
            column = multiple(chip // 2 % 2 * HD, HD)
            target = pl.ds(multiple(place * STRIPE, STRIPE), STRIPE)
            for kind, (source, there, send, recv) in enumerate(
                ((k_ref, kg, k_send, k_recv), (v_ref, vg, v_send, v_recv))
            ):
                push(
                    source.at[pl.ds(row, STRIPE), pl.ds(column, HD)],
                    there.at[target, pl.ds(0, HD)],
                    (2 * chip + kind, head), me, send.at[chip], recv,
                )
            return carry

        lax.fori_loop(0, CHIPS, send_keys, 0)

    def project(rows):
        return dot(rows, w_ref[...], CONTRACT_LAST).astype(BF16)

    part_row = lax.broadcasted_iota(jnp.int32, (SIDE, 64), 0)
    norm = n_ref[...].astype(F32) * (1.0 / SCALE)
    high = norm.astype(BF16).astype(F32)
    middle = (norm - high).astype(BF16).astype(F32)
    low = norm - high - middle
    for chunk in range(8):
        for h in range(2):
            cut = (slice(h, h + 1), slice(chunk * 64, (chunk + 1) * 64))
            rows = jnp.where(part_row == 0, high[cut], 0.0)
            rows = jnp.where(part_row == 1, middle[cut], rows)
            rows = jnp.where(part_row == 2, low[cut], rows)
            norms[chunk, h, :, 0:64] = rows

    def finish(chunk):
        rows = pl.ds(multiple(chunk * 64, 64), 64)
        for h in range(2):
            product = dl[chunk, h, 0:64, :].astype(F32) * o_ref[rows, h * HD:(h + 1) * HD].astype(F32)
            delta = jnp.sum(product.T, axis=0, keepdims=True).astype(BF16).astype(F32)
            extra = jnp.where(part_row == 3, delta, norms[chunk, h, :, 0:64])
            dl[chunk, h, 64:80, :] = jnp.concatenate(
                [extra, jnp.zeros((SIDE, 64), F32)], axis=1
            ).astype(BF16)

        def send(step, carry):
            index = lax.rem(me + step, 8)
            push(
                dl.at[chunk, index % 2],
                dg.at[own_slot, chunk, own_piece],
                (task_of(index), head), me, d_send.at[index], d_recv.at[chunk],
            )
            return carry

        lax.fori_loop(0, 8, send, 0)

    grad = project(g_ref[...])
    for h in range(2):
        dl[head, h, 0:64, :] = grad[:, h * HD:(h + 1) * HD]
    finish(head)

    kg[:, HD:] = pick(TASK_K, 0, 2)
    vg[:, HD:] = pick(TASK_K, 3, 3)
    dk_sum[...] = jnp.zeros_like(dk_sum)
    dv_sum[...] = jnp.zeros_like(dv_sum)
    in_group = lax.broadcasted_iota(jnp.int32, (32, HD), 0)

    def coarse_of(slot):
        return group + slot * (7 - 2 * group)

    def number_rows(index, carry):
        slot, chunk, half, pair = index // 32, index // 4 % 8, index // 2 % 2, index % 2
        pair = coarse_of(slot) * 32 + half * 16 + chunk * 2 + pair
        block = 2 * pair + jnp.where(in_group >= sizes[2 * pair], 1, 0)
        row = half * 64 + index % 2 * 32
        row_block[slot, chunk, pl.ds(multiple(row, 32), 32), :] = block
        row_block[slot, chunk, pl.ds(multiple(128 + row, 32), 32), :] = block + 1
        return carry

    lax.fori_loop(0, 64, number_rows, 0)
    row_lane = lax.broadcasted_iota(jnp.int32, (1, HD), 1)

    def number_keys(index, carry):
        blocks = []
        for half in range(2):
            pair = (index * 1024 + half * ROWS + x * STRIPE) // 32
            part = row_lane // 32
            size = jnp.where(
                part < 2,
                jnp.where(part == 0, sizes[2 * pair], sizes[2 * pair + 2]),
                jnp.where(part == 2, sizes[2 * pair + 4], sizes[2 * pair + 6]),
            )
            blocks.append(2 * (pair + part) + jnp.where(row_lane % 32 >= size, 1, 0))
        key_block[index] = jnp.concatenate(blocks, axis=1)
        return carry

    lax.fori_loop(0, 8, number_keys, 0)

    def query_owner(index):
        slot, kind, half = index // 4, index // 2 % 2, index % 2
        return kind * SHARDS + 2 * coarse_of(slot) + half

    def relay(there, recv):
        half = there.at[:, pl.ds(0, HD)]
        return pltpu.make_async_remote_copy(
            src_ref=half, dst_ref=half, send_sem=relay_send, recv_sem=recv,
            device_id=(sibling, head), device_id_type=MESH,
        )

    def attend(turn, carry):
        chunk = lax.rem(head + 8 + (turn + 1) // 2 * (1 - 2 * (turn % 2)), 8)

        @pl.when(turn == 0)
        def _():
            wait_bytes(qg, q_recv)
            for kind, (there, recv) in enumerate(((kg, k_recv), (vg, v_recv))):
                @pl.when(core == kind)
                def _():
                    wait_bytes(there.at[:, pl.ds(0, HD)], recv)
                    relay(there, recv).start()
            for kind, (there, recv) in enumerate(((vg, v_recv), (kg, k_recv))):
                @pl.when(core == kind)
                def _():
                    wait_bytes(there.at[:, pl.ds(0, HD)], recv)

        wait_bytes(dg.at[:, chunk], d_recv.at[chunk])
        dq_sum[...] = jnp.zeros_like(dq_sum)
        for slot in range(2):
            extras[slot] = side([dg[slot, chunk, piece, 64:80, :] for piece in range(4)])
        later = None
        for number in range(9):
            slot = 1 if number >= 4 else (number - group + 3) // 4
            pair = number - slot * (group + 1)
            keys = pl.ds(multiple(pair * 256, 256), 256)
            mask = None
            if number < 4 or number == 8:
                own = row_block[slot, chunk]
                mask = jnp.concatenate([own, own], axis=1) > key_block[pair]
            grads = dg[slot, chunk, :, 0:64, :].reshape(256, HD)
            dq, dk, dv = tile(qg[slot, chunk], grads, extras[slot], kg[keys, :], vg[keys, :], mask)
            dk_sum[keys, :] += dk
            dv_sum[keys, :] += dv
            if number < 4:
                dq_sum[slot] += dq
            else:
                later = dq if later is None else later + dq
        first = (dq_sum[0] * SCALE).astype(BF16)
        second = ((dq_sum[1] + later) * SCALE).astype(BF16)
        for index in range(8):
            part = (first, second)[index // 4]
            dq_part[chunk, index] = part[index % 4 * 64:(index % 4 + 1) * 64]

        def send(step, inner):
            index = lax.rem(me + step, 8)
            push(
                dq_part.at[chunk, index],
                rq.at[x, chunk, :, pl.ds(multiple(which * HD, HD), HD)],
                (query_owner(index), head), me, dq_send.at[index], dq_recv,
            )
            return inner

        lax.fori_loop(0, 8, send, 0)
        return carry

    def attended(step):
        return step // 4 * (2 * step - 7) + step // 7

    def step(index, carry):
        for direction in range(2):
            ring(direction, index, landed.at[index, direction]).wait_recv()

            @pl.when(index < 5)
            def _():
                ring(direction, lax.rem(index + 2, 7), landed.at[index, direction]).start()

        away = index // 2 + 1
        chunks = (lax.rem(head + 8 - away, 8), lax.rem(head + away, 8))
        units = (index % 2, 1 - index % 2)
        grad = project(landed[index].reshape(2 * UNIT, 4096))
        for direction in range(2):
            rows = pl.ds(multiple(units[direction] * UNIT, UNIT), UNIT)
            for h in range(2):
                dl[chunks[direction], h, rows, :] = grad[
                    direction * UNIT:(direction + 1) * UNIT, h * HD:(h + 1) * HD
                ]

        @pl.when(index % 2 == 1)
        def _():
            finish(chunks[0])

        @pl.when((index % 2 == 1) | (index == 6))
        def _():
            finish(chunks[1])

        lax.fori_loop(attended(index), attended(index + 1), attend, 0)
        return carry

    lax.fori_loop(0, 7, step, 0)

    def narrow(index, carry):
        there = pl.ds(multiple(index * 256 + (1 - core) * STRIPE, STRIPE), STRIPE)
        to_sibling[0, index] = (dk_sum[there, :] * SCALE).astype(BF16)
        to_sibling[1, index] = dv_sum[there, :].astype(BF16)
        return carry

    lax.fori_loop(0, 8, narrow, 0)
    across = pltpu.make_async_remote_copy(
        src_ref=to_sibling, dst_ref=from_sibling, send_sem=sibling_send, recv_sem=sibling_recv,
        device_id=(sibling, head), device_id_type=MESH,
    )
    across.start()
    across.wait_recv()

    def pass_on(step, carry):
        index = lax.rem(me // 2 + step, 8)
        here = pl.ds(multiple(index * 256 + core * STRIPE, STRIPE), STRIPE)
        key_part[index, 0] = (
            dk_sum[here, :] * SCALE + from_sibling[0, index].astype(F32)
        ).astype(BF16)
        key_part[index, 1] = (dv_sum[here, :] + from_sibling[1, index].astype(F32)).astype(BF16)
        push(
            key_part.at[index],
            rk.at[y % 2, :, pl.ds(multiple(x * STRIPE, STRIPE), STRIPE), pl.ds(multiple(which * HD, HD), HD)],
            (SHARDS + 2 * index + core, head), me, part_send.at[index], part_recv,
        )
        return carry

    lax.fori_loop(0, 8, pass_on, 0)

    @pl.when(me < SHARDS)
    def _():
        def number_own(index, carry):
            pair = place * 16 + index
            own_block[pl.ds(multiple(index * 32, 32), 32), :] = 2 * pair + jnp.where(
                in_group >= sizes[2 * pair], 1, 0
            )
            return carry

        lax.fori_loop(0, 16, number_own, 0)
        for part in range(4):
            rows = slice(part * STRIPE, (part + 1) * STRIPE)
            block = own_block[rows, :].astype(F32)
            mask = block == block.T
            for h in range(2):
                columns = slice(h * HD, (h + 1) * HD)
                dq, dk, dv = tile(
                    q_ref[2 * part:2 * part + 2, :, columns].reshape(STRIPE, HD),
                    dl[2 * part:2 * part + 2, h, 0:64, :].reshape(STRIPE, HD),
                    side([dl[2 * part + number, h, 64:80, :] for number in range(2)]),
                    jnp.concatenate([k_ref[rows, columns], pick(STRIPE, 0, 2)], axis=1),
                    jnp.concatenate([v_ref[rows, columns], pick(STRIPE, 3, 3)], axis=1),
                    mask,
                )
                dq_own[rows, columns] = dq * SCALE
                dk_out[rows, columns] = (dk * SCALE).astype(BF16)
                dv_out[rows, columns] = dv.astype(BF16)

    wait_bytes(rq, dq_recv)

    def summed_queries():
        parts = [rq[stripe].reshape(ROWS, 256).astype(F32) for stripe in range(4)]
        return (parts[0] + parts[1]) + (parts[2] + parts[3])

    @pl.when(me < SHARDS)
    def _():
        dq_out[...] = (summed_queries() + dq_own[...]).astype(BF16)

    @pl.when(clean)
    def _():
        dq_out[...] = summed_queries().astype(BF16)
        wait_bytes(rk, part_recv)
        dk_out[...] = (rk[0, 0].astype(F32) + rk[1, 0].astype(F32)).astype(BF16)
        dv_out[...] = (rk[0, 1].astype(F32) + rk[1, 1].astype(F32)).astype(BF16)

    for index in range(7):
        for direction in range(2):
            ring(direction, index, landed.at[index, direction]).wait_send()
    across.wait_send()
    relay(kg, k_recv).wait_send()

    def settle(index, carry):
        @pl.when(task_of(index) != me)
        def _():
            wait_bytes(q_ref.at[:, :, pl.ds(0, HD)], q_send.at[index])
            wait_bytes(dl.at[:, 0], d_send.at[index])

        @pl.when(query_owner(index) != me)
        def _():
            wait_bytes(dq_part.at[:, index], dq_send.at[index])

        @pl.when(SHARDS + 2 * index + core != me)
        def _():
            wait_bytes(key_part.at[index], part_send.at[index])
        return carry

    lax.fori_loop(0, 8, settle, 0)

    @pl.when(clean)
    def _():
        def settle_keys(chip, carry):
            for kind, (source, send) in enumerate(((k_ref, k_send), (v_ref, v_send))):
                @pl.when(2 * chip + kind != me)
                def _():
                    wait_bytes(source.at[pl.ds(0, STRIPE), pl.ds(0, HD)], send.at[chip])
            return carry

        lax.fori_loop(0, CHIPS, settle_keys, 0)


VMEM = pl.BlockSpec(memory_space=pltpu.VMEM)
SMEM = pl.BlockSpec(memory_space=pltpu.SMEM)
DMA = pltpu.SemaphoreType.DMA
LIMIT = 56 * 1024 * 1024


def shards(queries, keys, values, attn_out, out_grad, out_weight, log_norm, block_sizes):
    return pl.pallas_call(
        layer_kernel,
        name="layer",
        out_shape=(jax.ShapeDtypeStruct((ROWS, 256), BF16),) * 3,
        in_specs=[SMEM] + [VMEM] * 7,
        out_specs=(VMEM,) * 3,
        scratch_shapes=[
            pltpu.VMEM((7, 2, UNIT, 4096), BF16),
            pltpu.VMEM((2, 8, 256, HD), BF16),
            pltpu.VMEM((2, 8, 4, 64 + SIDE, HD), BF16),
            pltpu.VMEM((TASK_K, 256), BF16),
            pltpu.VMEM((TASK_K, 256), BF16),
            pltpu.VMEM((8, 2, 64 + SIDE, HD), BF16),
            pltpu.VMEM((8, 2, SIDE, HD), F32),
            pltpu.VMEM((2, 256, HD), BF16),
            pltpu.VMEM((2, 256, HD), F32),
            pltpu.VMEM((TASK_K, HD), F32),
            pltpu.VMEM((TASK_K, HD), F32),
            pltpu.VMEM((2, 8, 256, HD), jnp.int32),
            pltpu.VMEM((8, 1, 256), jnp.int32),
            pltpu.VMEM((ROWS, HD), jnp.int32),
            pltpu.VMEM((ROWS, 256), F32),
            pltpu.VMEM((8, 8, 64, HD), BF16),
            pltpu.VMEM((2, 8, STRIPE, HD), BF16),
            pltpu.VMEM((2, 8, STRIPE, HD), BF16),
            pltpu.VMEM((8, 2, STRIPE, HD), BF16),
            pltpu.VMEM((4, 8, 64, 256), BF16),
            pltpu.VMEM((2, 2, ROWS, 256), BF16),
            DMA((2, 7)), DMA((2, 7)), DMA((8,)), DMA((CHIPS,)), DMA((CHIPS,)), DMA((8,)),
            DMA, DMA, DMA, DMA((8,)),
            DMA((8,)), DMA, DMA, DMA, DMA((8,)), DMA, DMA,
        ],
        compiler_params=pltpu.CompilerParams(
            collective_id=0, has_side_effects=True, vmem_limit_bytes=LIMIT
        ),
    )(
        block_sizes, queries.reshape(8, 64, 256), keys, values, attn_out, out_grad, out_weight,
        log_norm.T,
    )


def solution(mesh):
    in_specs = (
        P("seq", "head"),
        P("seq", "head"),
        P("seq", "head"),
        P("seq", "head"),
        P(("seq", "head"), None),
        P("head", None),
        P("seq", "head"),
        P(),
    )
    out_specs = (P("seq", "head"), P("seq", "head"), P("seq", "head"))
    return jax.shard_map(shards, mesh=mesh, in_specs=in_specs, out_specs=out_specs, check_vma=False)
```

```python
import functools
import math

import jax
import jax.numpy as jnp
from jax import lax
from jax.experimental import pallas as pl
from jax.experimental.pallas import tpu as pltpu
from jax.sharding import PartitionSpec as P

HD = 128
UNIT = 32
HALF_UNIT = 16
SIDE = 16
ROWS = 512
STRIPE = 128
TASK_K = 2048
PEERS = 32
SHARDS = 16
CHIPS = 16
SCALE = HD ** -0.5
MESH = pl.DeviceIdType.MESH
F32 = jnp.float32
BF16 = jnp.bfloat16
CONTRACT = (((1,), (0,)), ((), ()))
CONTRACT_LAST = (((1,), (1,)), ((), ()))
CONTRACT_FIRST = (((0,), (0,)), ((), ()))


def where_am_i():
    seq = lax.axis_index("seq")
    return seq, seq // 8, (seq // 2) % 4, seq % 2


def multiple(value, of):
    return pl.multiple_of(value, of)


def push(here, there, device, me, send_sem, recv_sem):
    seq, head = device

    @pl.when(seq == me)
    def _():
        pltpu.make_async_copy(here, there, recv_sem).start()

    @pl.when(seq != me)
    def _():
        pltpu.make_async_remote_copy(
            src_ref=here, dst_ref=there, send_sem=send_sem, recv_sem=recv_sem,
            device_id=(seq, head), device_id_type=MESH,
        ).start()


def wait_bytes(ref, sem):
    pltpu.make_async_copy(ref, ref, sem).wait()


def dot(a, b, dims):
    return lax.dot_general(a, b, dims, preferred_element_type=F32)


def tile(q, d, turned_q, turned_d, extra, keys, values, mask):
    score = dot(jnp.concatenate([q, extra], axis=1), keys, CONTRACT_LAST)
    probs = jnp.exp2(score * (SCALE * math.log2(math.e)))
    if mask is not None:
        probs = jnp.where(mask, probs, 0.0)
    grad = (probs * dot(jnp.concatenate([d, extra], axis=1), values, CONTRACT_LAST)).astype(BF16)
    dq = dot(grad, keys[:, :HD], CONTRACT)
    dk = dot(turned_q, grad, CONTRACT)
    dv = dot(turned_d, probs.astype(BF16), CONTRACT)
    return dq, dk, dv


def pick(rows, first, last):
    lane = lax.broadcasted_iota(jnp.int32, (rows, HD), 1)
    part = lane % SIDE
    return jnp.where((lane < 4 * SIDE) & (part >= first) & (part <= last), -1.0, 0.0).astype(BF16)


def side(pieces):
    stacked = jnp.concatenate([piece.astype(F32) for piece in pieces], axis=0)
    filler = jnp.zeros((HD - stacked.shape[0], HD), F32)
    turned = jnp.concatenate([stacked, filler], axis=0).T[:64]
    lane = lax.broadcasted_iota(jnp.int32, (64, HD), 1)
    return jnp.concatenate(
        [jnp.where(lane // SIDE == number, turned, 0.0) for number in range(len(pieces))], axis=0
    ).astype(BF16)


def layer_kernel(
    sizes, q_ref, k_ref, v_ref, g_hbm, w_hbm, o_ref, n_ref,
    dq_out, dk_out, dv_out,
    g_ref, w_ref, q_own, k_own, v_own,
    landed, qg, dg, kg, vg, dl, norms, extras, turned,
    dq_sum, dk_sum, dv_sum, row_block, key_block, own_block, dq_own,
    dq_part, to_sibling, from_sibling, key_part, rq, rk,
    ring_send, ring_recv, q_send, k_send, v_send, d_send, q_recv, k_recv, v_recv, d_recv,
    dq_send, dq_recv, sibling_send, sibling_recv, part_send, part_recv, relay_send, fetch,
):
    me, x, y, core = where_am_i()
    head = lax.axis_index("head")
    right, left = lax.rem(head + 1, 8), lax.rem(head + 7, 8)
    place = me % SHARDS
    clean = me >= SHARDS
    own_slot = x % 2
    own_group = y + own_slot * (3 - 2 * y)
    own_piece = (x // 2) * 2 + core
    group = core * 2 + y % 2
    which = y // 2
    sibling = me + 1 - 2 * core

    fetches = [
        pltpu.make_async_copy(source, target, fetch.at[number])
        for number, (source, target) in enumerate(
            ((g_hbm, g_ref), (w_hbm, w_ref), (q_ref, q_own), (k_ref, k_own), (v_ref, v_own))
        )
    ]
    for number in range(2):
        fetches[number].start()

    barrier = pltpu.get_barrier_semaphore()

    def greet(step, carry):
        pl.semaphore_signal(
            barrier, inc=1, device_id=(lax.rem(me + step, PEERS), head), device_id_type=MESH
        )
        return carry

    lax.fori_loop(1, PEERS, greet, 0)
    for neighbour in (left, right):
        pl.semaphore_signal(barrier, inc=1, device_id=(me, neighbour), device_id_type=MESH)
    pl.semaphore_wait(barrier, PEERS + 1)

    def ring(direction, index, sub, source):
        rows = pl.ds(sub * HALF_UNIT, HALF_UNIT)
        return pltpu.make_async_remote_copy(
            src_ref=source.at[rows],
            dst_ref=landed.at[index, direction, rows],
            send_sem=ring_send.at[direction, index, sub],
            recv_sem=ring_recv.at[direction, index, sub],
            device_id=(me, (right, left)[direction]),
            device_id_type=MESH,
        )

    for index in range(2):
        for sub in range(2):
            for direction in range(2):
                unit = index if direction == 0 else 1 - index
                ring(direction, index, sub, g_hbm.at[pl.ds(unit * UNIT, UNIT)]).start()

    def task_of(index):
        stripe, part = index // 2, index % 2
        return (stripe * 4 + 2 * part + own_group % 2) * 2 + own_group // 2

    def send_queries(step, carry):
        index = lax.rem(me + step, 8)
        column = multiple(index % 2 * HD, HD)
        push(
            q_ref.at[:, :, pl.ds(column, HD)],
            qg.at[own_slot, :, pl.ds(multiple(own_piece * 64, 64), 64)],
            (task_of(index), head), me, q_send.at[index], q_recv,
        )
        return carry

    lax.fori_loop(0, 8, send_queries, 0)

    @pl.when(clean)
    def _():
        def send_keys(step, carry):
            chip = lax.rem(me // 2 + step, CHIPS)
            row = multiple(chip // 4 * STRIPE, STRIPE)
            column = multiple(chip // 2 % 2 * HD, HD)
            target = pl.ds(multiple(place * STRIPE, STRIPE), STRIPE)
            for kind, (source, there, send, recv) in enumerate(
                ((k_ref, kg, k_send, k_recv), (v_ref, vg, v_send, v_recv))
            ):
                push(
                    source.at[pl.ds(row, STRIPE), pl.ds(column, HD)],
                    there.at[target, pl.ds(0, HD)],
                    (2 * chip + kind, head), me, send.at[chip], recv,
                )
            return carry

        lax.fori_loop(0, CHIPS, send_keys, 0)

    def project(rows):
        return dot(rows, w_ref[...], CONTRACT_LAST).astype(BF16)

    part_row = lax.broadcasted_iota(jnp.int32, (SIDE, 64), 0)
    norm = n_ref[...].astype(F32) * (1.0 / SCALE)
    high = norm.astype(BF16).astype(F32)
    middle = (norm - high).astype(BF16).astype(F32)
    low = norm - high - middle
    for chunk in range(8):
        for h in range(2):
            cut = (slice(h, h + 1), slice(chunk * 64, (chunk + 1) * 64))
            rows = jnp.where(part_row == 0, high[cut], 0.0)
            rows = jnp.where(part_row == 1, middle[cut], rows)
            rows = jnp.where(part_row == 2, low[cut], rows)
            norms[chunk, h, :, 0:64] = rows

    def finish(chunk):
        rows = pl.ds(multiple(chunk * 64, 64), 64)
        for h in range(2):
            product = dl[chunk, h, 0:64, :].astype(F32) * o_ref[rows, h * HD:(h + 1) * HD].astype(F32)
            delta = jnp.sum(product.T, axis=0, keepdims=True).astype(BF16).astype(F32)
            extra = jnp.where(part_row == 3, delta, norms[chunk, h, :, 0:64])
            dl[chunk, h, 64:80, :] = jnp.concatenate(
                [extra, jnp.zeros((SIDE, 64), F32)], axis=1
            ).astype(BF16)

        def send(step, carry):
            index = lax.rem(me + step, 8)
            push(
                dl.at[chunk, index % 2],
                dg.at[own_slot, chunk, own_piece],
                (task_of(index), head), me, d_send.at[index], d_recv.at[chunk],
            )
            return carry

        lax.fori_loop(0, 8, send, 0)

    for number in range(2):
        fetches[number].wait()
    for number in range(2, 5):
        fetches[number].start()
    grad = project(g_ref[...])
    for h in range(2):
        dl[head, h, 0:64, :] = grad[:, h * HD:(h + 1) * HD]
    finish(head)

    kg[:, HD:] = pick(TASK_K, 0, 2)
    vg[:, HD:] = pick(TASK_K, 3, 3)
    dk_sum[...] = jnp.zeros_like(dk_sum)
    dv_sum[...] = jnp.zeros_like(dv_sum)
    in_group = lax.broadcasted_iota(jnp.int32, (32, HD), 0)

    def coarse_of(slot):
        return group + slot * (7 - 2 * group)

    def number_rows(index, carry):
        slot, chunk, half, pair = index // 32, index // 4 % 8, index // 2 % 2, index % 2
        pair = coarse_of(slot) * 32 + half * 16 + chunk * 2 + pair
        block = 2 * pair + jnp.where(in_group >= sizes[2 * pair], 1, 0)
        row = half * 64 + index % 2 * 32
        row_block[slot, chunk, pl.ds(multiple(row, 32), 32), :] = block
        row_block[slot, chunk, pl.ds(multiple(128 + row, 32), 32), :] = block + 1
        return carry

    lax.fori_loop(0, 64, number_rows, 0)
    row_lane = lax.broadcasted_iota(jnp.int32, (1, HD), 1)

    def number_keys(index, carry):
        blocks = []
        for half in range(2):
            pair = (index * 1024 + half * ROWS + x * STRIPE) // 32
            part = row_lane // 32
            size = jnp.where(
                part < 2,
                jnp.where(part == 0, sizes[2 * pair], sizes[2 * pair + 2]),
                jnp.where(part == 2, sizes[2 * pair + 4], sizes[2 * pair + 6]),
            )
            blocks.append(2 * (pair + part) + jnp.where(row_lane % 32 >= size, 1, 0))
        key_block[index] = jnp.concatenate(blocks, axis=1)
        return carry

    lax.fori_loop(0, 8, number_keys, 0)

    def query_owner(index):
        slot, kind, half = index // 4, index // 2 % 2, index % 2
        return kind * SHARDS + 2 * coarse_of(slot) + half

    def relay(there, recv):
        half = there.at[:, pl.ds(0, HD)]
        return pltpu.make_async_remote_copy(
            src_ref=half, dst_ref=half, send_sem=relay_send, recv_sem=recv,
            device_id=(sibling, head), device_id_type=MESH,
        )

    def attend(turn, carry):
        chunk = lax.rem(head + 8 + (turn + 1) // 2 * (1 - 2 * (turn % 2)), 8)

        @pl.when(turn == 0)
        def _():
            wait_bytes(qg, q_recv)
            for kind, (there, recv) in enumerate(((kg, k_recv), (vg, v_recv))):
                @pl.when(core == kind)
                def _():
                    wait_bytes(there.at[:, pl.ds(0, HD)], recv)
                    relay(there, recv).start()
            for kind, (there, recv) in enumerate(((vg, v_recv), (kg, k_recv))):
                @pl.when(core == kind)
                def _():
                    wait_bytes(there.at[:, pl.ds(0, HD)], recv)

        wait_bytes(dg.at[:, chunk], d_recv.at[chunk])
        dq_sum[...] = jnp.zeros_like(dq_sum)
        for slot in range(2):
            extras[slot] = side([dg[slot, chunk, piece, 64:80, :] for piece in range(4)])
            turned[slot, 0] = qg[slot, chunk].T
            turned[slot, 1] = dg[slot, chunk, :, 0:64, :].reshape(256, HD).T
        later = None
        for number in range(9):
            slot = 1 if number >= 4 else (number - group + 3) // 4
            pair = number - slot * (group + 1)
            keys = pl.ds(multiple(pair * 256, 256), 256)
            mask = None
            if number < 4 or number == 8:
                own = row_block[slot, chunk]
                mask = jnp.concatenate([own, own], axis=1) > key_block[pair]
            grads = dg[slot, chunk, :, 0:64, :].reshape(256, HD)
            dq, dk, dv = tile(
                qg[slot, chunk], grads, turned[slot, 0], turned[slot, 1], extras[slot],
                kg[keys, :], vg[keys, :], mask,
            )
            dk_sum[pair] += dk
            dv_sum[pair] += dv
            if number < 4:
                dq_sum[slot] += dq
            else:
                later = dq if later is None else later + dq
        first = (dq_sum[0] * SCALE).astype(BF16)
        second = ((dq_sum[1] + later) * SCALE).astype(BF16)
        for index in range(8):
            part = (first, second)[index // 4]
            dq_part[chunk, index] = part[index % 4 * 64:(index % 4 + 1) * 64]

        def send(step, inner):
            index = lax.rem(me + step, 8)
            push(
                dq_part.at[chunk, index],
                rq.at[x, chunk, :, pl.ds(multiple(which * HD, HD), HD)],
                (query_owner(index), head), me, dq_send.at[index], dq_recv,
            )
            return inner

        lax.fori_loop(0, 8, send, 0)
        return carry

    def attended(step):
        return step // 4 * (2 * step - 7) + step // 7

    def step(index, carry):
        for sub in range(2):
            for direction in range(2):
                source = landed.at[index, direction]
                ring(direction, index, sub, source).wait_recv()

                @pl.when(index < 5)
                def _():
                    ring(direction, lax.rem(index + 2, 7), sub, source).start()

        away = index // 2 + 1
        chunks = (lax.rem(head + 8 - away, 8), lax.rem(head + away, 8))
        units = (index % 2, 1 - index % 2)
        grad = project(landed[index].reshape(2 * UNIT, 4096))
        for direction in range(2):
            rows = pl.ds(multiple(units[direction] * UNIT, UNIT), UNIT)
            for h in range(2):
                dl[chunks[direction], h, rows, :] = grad[
                    direction * UNIT:(direction + 1) * UNIT, h * HD:(h + 1) * HD
                ]

        @pl.when(index % 2 == 1)
        def _():
            finish(chunks[0])

        @pl.when((index % 2 == 1) | (index == 6))
        def _():
            finish(chunks[1])

        lax.fori_loop(attended(index), attended(index + 1), attend, 0)
        return carry

    lax.fori_loop(0, 7, step, 0)

    def narrow(index, carry):
        there = pl.ds(multiple((1 - core) * STRIPE, STRIPE), STRIPE)
        to_sibling[0, index] = (dk_sum[index, :, there] * SCALE).T.astype(BF16)
        to_sibling[1, index] = dv_sum[index, :, there].T.astype(BF16)
        return carry

    lax.fori_loop(0, 8, narrow, 0)
    across = pltpu.make_async_remote_copy(
        src_ref=to_sibling, dst_ref=from_sibling, send_sem=sibling_send, recv_sem=sibling_recv,
        device_id=(sibling, head), device_id_type=MESH,
    )
    across.start()
    across.wait_recv()

    def pass_on(step, carry):
        index = lax.rem(me // 2 + step, 8)
        here = pl.ds(multiple(core * STRIPE, STRIPE), STRIPE)
        key_part[index, 0] = (
            (dk_sum[index, :, here] * SCALE).T + from_sibling[0, index].astype(F32)
        ).astype(BF16)
        key_part[index, 1] = (
            dv_sum[index, :, here].T + from_sibling[1, index].astype(F32)
        ).astype(BF16)
        push(
            key_part.at[index],
            rk.at[y % 2, :, pl.ds(multiple(x * STRIPE, STRIPE), STRIPE), pl.ds(multiple(which * HD, HD), HD)],
            (SHARDS + 2 * index + core, head), me, part_send.at[index], part_recv,
        )
        return carry

    lax.fori_loop(0, 8, pass_on, 0)

    for number in range(2, 5):
        fetches[number].wait()

    @pl.when(me < SHARDS)
    def _():
        def number_own(index, carry):
            pair = place * 16 + index
            own_block[pl.ds(multiple(index * 32, 32), 32), :] = 2 * pair + jnp.where(
                in_group >= sizes[2 * pair], 1, 0
            )
            return carry

        lax.fori_loop(0, 16, number_own, 0)
        for part in range(4):
            rows = slice(part * STRIPE, (part + 1) * STRIPE)
            block = own_block[rows, :].astype(F32)
            mask = block == block.T
            for h in range(2):
                columns = slice(h * HD, (h + 1) * HD)
                own_q = q_own[2 * part:2 * part + 2, :, columns].reshape(STRIPE, HD)
                own_d = dl[2 * part:2 * part + 2, h, 0:64, :].reshape(STRIPE, HD)
                dq, dk, dv = tile(
                    own_q, own_d, own_q.T, own_d.T,
                    side([dl[2 * part + number, h, 64:80, :] for number in range(2)]),
                    jnp.concatenate([k_own[rows, columns], pick(STRIPE, 0, 2)], axis=1),
                    jnp.concatenate([v_own[rows, columns], pick(STRIPE, 3, 3)], axis=1),
                    mask,
                )
                dq_own[rows, columns] = dq * SCALE
                dk_out[rows, columns] = (dk * SCALE).T.astype(BF16)
                dv_out[rows, columns] = dv.T.astype(BF16)

    wait_bytes(rq, dq_recv)

    def summed_queries():
        parts = [rq[stripe].reshape(ROWS, 256).astype(F32) for stripe in range(4)]
        return (parts[0] + parts[1]) + (parts[2] + parts[3])

    @pl.when(me < SHARDS)
    def _():
        dq_out[...] = (summed_queries() + dq_own[...]).astype(BF16)

    @pl.when(clean)
    def _():
        dq_out[...] = summed_queries().astype(BF16)
        wait_bytes(rk, part_recv)
        dk_out[...] = (rk[0, 0].astype(F32) + rk[1, 0].astype(F32)).astype(BF16)
        dv_out[...] = (rk[0, 1].astype(F32) + rk[1, 1].astype(F32)).astype(BF16)

    for index in range(7):
        for direction in range(2):
            for sub in range(2):
                ring(direction, index, sub, landed.at[index, direction]).wait_send()
    across.wait_send()
    relay(kg, k_recv).wait_send()

    def settle(index, carry):
        @pl.when(task_of(index) != me)
        def _():
            wait_bytes(q_ref.at[:, :, pl.ds(0, HD)], q_send.at[index])
            wait_bytes(dl.at[:, 0], d_send.at[index])

        @pl.when(query_owner(index) != me)
        def _():
            wait_bytes(dq_part.at[:, index], dq_send.at[index])

        @pl.when(SHARDS + 2 * index + core != me)
        def _():
            wait_bytes(key_part.at[index], part_send.at[index])
        return carry

    lax.fori_loop(0, 8, settle, 0)

    @pl.when(clean)
    def _():
        def settle_keys(chip, carry):
            for kind, (source, send) in enumerate(((k_ref, k_send), (v_ref, v_send))):
                @pl.when(2 * chip + kind != me)
                def _():
                    wait_bytes(source.at[pl.ds(0, STRIPE), pl.ds(0, HD)], send.at[chip])
            return carry

        lax.fori_loop(0, CHIPS, settle_keys, 0)


ANY = pl.BlockSpec(memory_space=pl.ANY)
VMEM = pl.BlockSpec(memory_space=pltpu.VMEM)
SMEM = pl.BlockSpec(memory_space=pltpu.SMEM)
DMA = pltpu.SemaphoreType.DMA
LIMIT = 56 * 1024 * 1024


def hand_on_kernel(*refs):
    for source, target in zip(refs[:3], refs[3:]):
        target[...] = source[...]


def hand_on(results):
    return pl.pallas_call(
        hand_on_kernel,
        name="hand_on",
        out_shape=(jax.ShapeDtypeStruct((ROWS, 256), BF16),) * 3,
        in_specs=[VMEM] * 3,
        out_specs=(VMEM,) * 3,
        compiler_params=pltpu.CompilerParams(vmem_limit_bytes=LIMIT),
    )(*results)


def shards(queries, keys, values, attn_out, out_grad, out_weight, log_norm, block_sizes):
    results = pl.pallas_call(
        layer_kernel,
        name="layer",
        out_shape=(jax.ShapeDtypeStruct((ROWS, 256), BF16),) * 3,
        in_specs=[SMEM] + [ANY] * 5 + [VMEM] * 2,
        out_specs=(VMEM,) * 3,
        scratch_shapes=[
            pltpu.VMEM((64, 4096), BF16),
            pltpu.VMEM((256, 4096), BF16),
            pltpu.VMEM((8, 64, 256), BF16),
            pltpu.VMEM((ROWS, 256), BF16),
            pltpu.VMEM((ROWS, 256), BF16),
            pltpu.VMEM((7, 2, UNIT, 4096), BF16),
            pltpu.VMEM((2, 8, 256, HD), BF16),
            pltpu.VMEM((2, 8, 4, 64 + SIDE, HD), BF16),
            pltpu.VMEM((TASK_K, 256), BF16),
            pltpu.VMEM((TASK_K, 256), BF16),
            pltpu.VMEM((8, 2, 64 + SIDE, HD), BF16),
            pltpu.VMEM((8, 2, SIDE, HD), F32),
            pltpu.VMEM((2, 256, HD), BF16),
            pltpu.VMEM((2, 2, HD, 256), BF16),
            pltpu.VMEM((2, 256, HD), F32),
            pltpu.VMEM((8, HD, 256), F32),
            pltpu.VMEM((8, HD, 256), F32),
            pltpu.VMEM((2, 8, 256, HD), jnp.int32),
            pltpu.VMEM((8, 1, 256), jnp.int32),
            pltpu.VMEM((ROWS, HD), jnp.int32),
            pltpu.VMEM((ROWS, 256), F32),
            pltpu.VMEM((8, 8, 64, HD), BF16),
            pltpu.VMEM((2, 8, STRIPE, HD), BF16),
            pltpu.VMEM((2, 8, STRIPE, HD), BF16),
            pltpu.VMEM((8, 2, STRIPE, HD), BF16),
            pltpu.VMEM((4, 8, 64, 256), BF16),
            pltpu.VMEM((2, 2, ROWS, 256), BF16),
            DMA((2, 7, 2)), DMA((2, 7, 2)), DMA((8,)), DMA((CHIPS,)), DMA((CHIPS,)), DMA((8,)),
            DMA, DMA, DMA, DMA((8,)),
            DMA((8,)), DMA, DMA, DMA, DMA((8,)), DMA, DMA, DMA((5,)),
        ],
        compiler_params=pltpu.CompilerParams(
            collective_id=0, has_side_effects=True, vmem_limit_bytes=LIMIT
        ),
    )(
        block_sizes, queries.reshape(8, 64, 256), keys, values, out_grad, out_weight, attn_out,
        log_norm.T,
    )
    return hand_on(results)


def solution(mesh):
    in_specs = (
        P("seq", "head"),
        P("seq", "head"),
        P("seq", "head"),
        P("seq", "head"),
        P(("seq", "head"), None),
        P("head", None),
        P("seq", "head"),
        P(),
    )
    out_specs = (P("seq", "head"), P("seq", "head"), P("seq", "head"))
    return jax.shard_map(shards, mesh=mesh, in_specs=in_specs, out_specs=out_specs, check_vma=False)
```

```python
import functools
import math

import jax
import jax.numpy as jnp
from jax import lax
from jax.experimental import pallas as pl
from jax.experimental.pallas import tpu as pltpu
from jax.sharding import PartitionSpec as P

HD = 128
UNIT = 32
HALF_UNIT = 16
SIDE = 16
ROWS = 512
STRIPE = 128
TASK_K = 2048
PEERS = 32
SHARDS = 16
CHIPS = 16
SCALE = HD ** -0.5
MESH = pl.DeviceIdType.MESH
F32 = jnp.float32
BF16 = jnp.bfloat16
CONTRACT = (((1,), (0,)), ((), ()))
CONTRACT_LAST = (((1,), (1,)), ((), ()))
CONTRACT_FIRST = (((0,), (0,)), ((), ()))


def where_am_i():
    seq = lax.axis_index("seq")
    return seq, seq // 8, (seq // 2) % 4, seq % 2


def multiple(value, of):
    return pl.multiple_of(value, of)


def push(here, there, device, me, send_sem, recv_sem):
    seq, head = device

    @pl.when(seq == me)
    def _():
        pltpu.make_async_copy(here, there, recv_sem).start()

    @pl.when(seq != me)
    def _():
        pltpu.make_async_remote_copy(
            src_ref=here, dst_ref=there, send_sem=send_sem, recv_sem=recv_sem,
            device_id=(seq, head), device_id_type=MESH,
        ).start()


def wait_bytes(ref, sem):
    pltpu.make_async_copy(ref, ref, sem).wait()


def dot(a, b, dims):
    return lax.dot_general(a, b, dims, preferred_element_type=F32)


def tile(q, d, turned_q, turned_d, extra, keys, values, mask):
    score = dot(jnp.concatenate([q, extra], axis=1), keys, CONTRACT_LAST)
    probs = jnp.exp2(score * (SCALE * math.log2(math.e)))
    if mask is not None:
        probs = jnp.where(mask, probs, 0.0)
    grad = (probs * dot(jnp.concatenate([d, extra], axis=1), values, CONTRACT_LAST)).astype(BF16)
    dq = dot(grad, keys[:, :HD], CONTRACT)
    dk = dot(turned_q, grad, CONTRACT)
    dv = dot(turned_d, probs.astype(BF16), CONTRACT)
    return dq, dk, dv


def pick(rows, first, last):
    lane = lax.broadcasted_iota(jnp.int32, (rows, HD), 1)
    part = lane % SIDE
    return jnp.where((lane < 4 * SIDE) & (part >= first) & (part <= last), -1.0, 0.0).astype(BF16)


def side(pieces):
    stacked = jnp.concatenate([piece.astype(F32) for piece in pieces], axis=0)
    filler = jnp.zeros((HD - stacked.shape[0], HD), F32)
    turned = jnp.concatenate([stacked, filler], axis=0).T[:64]
    lane = lax.broadcasted_iota(jnp.int32, (64, HD), 1)
    return jnp.concatenate(
        [jnp.where(lane // SIDE == number, turned, 0.0) for number in range(len(pieces))], axis=0
    ).astype(BF16)


def layer_kernel(
    sizes, q_ref, k_ref, v_ref, g_hbm, w_hbm, o_ref, n_ref,
    dq_out, dk_out, dv_out,
    g_ref, w_ref, q_own, k_own, v_own,
    landed, qg, dg, kg, vg, dl, norms, extras, turned,
    dq_sum, dk_sum, dv_sum, row_block, key_block, own_block, dq_own,
    dq_part, to_sibling, from_sibling, key_part, rq, rk,
    ring_send, ring_recv, q_send, k_send, v_send, d_send, q_recv, k_recv, v_recv, d_recv,
    dq_send, dq_recv, sibling_send, sibling_recv, part_send, part_recv, relay_send, fetch,
):
    me, x, y, core = where_am_i()
    head = lax.axis_index("head")
    right, left = lax.rem(head + 1, 8), lax.rem(head + 7, 8)
    place = me % SHARDS
    clean = me >= SHARDS
    own_slot = x % 2
    own_group = y + own_slot * (3 - 2 * y)
    own_piece = (x // 2) * 2 + core
    group = core * 2 + y % 2
    which = y // 2
    sibling = me + 1 - 2 * core

    fetches = [
        pltpu.make_async_copy(source, target, fetch.at[number])
        for number, (source, target) in enumerate(
            ((g_hbm, g_ref), (w_hbm, w_ref), (q_ref, q_own), (k_ref, k_own), (v_ref, v_own))
        )
    ]
    for number in range(2):
        fetches[number].start()

    barrier = pltpu.get_barrier_semaphore()

    def greet(step, carry):
        pl.semaphore_signal(
            barrier, inc=1, device_id=(lax.rem(me + step, PEERS), head), device_id_type=MESH
        )
        return carry

    lax.fori_loop(1, PEERS, greet, 0)
    for neighbour in (left, right):
        pl.semaphore_signal(barrier, inc=1, device_id=(me, neighbour), device_id_type=MESH)
    pl.semaphore_wait(barrier, PEERS + 1)

    def ring(direction, index, sub, source):
        rows = pl.ds(sub * HALF_UNIT, HALF_UNIT)
        return pltpu.make_async_remote_copy(
            src_ref=source.at[rows],
            dst_ref=landed.at[index, direction, rows],
            send_sem=ring_send.at[direction, index, sub],
            recv_sem=ring_recv.at[direction, index, sub],
            device_id=(me, (right, left)[direction]),
            device_id_type=MESH,
        )

    for index in range(2):
        for sub in range(2):
            for direction in range(2):
                unit = index if direction == 0 else 1 - index
                ring(direction, index, sub, g_hbm.at[pl.ds(unit * UNIT, UNIT)]).start()

    def task_of(index):
        stripe, part = index // 2, index % 2
        return (stripe * 4 + 2 * part + own_group % 2) * 2 + own_group // 2

    def send_queries(step, carry):
        index = lax.rem(me + step, 8)
        column = multiple(index % 2 * HD, HD)
        push(
            q_ref.at[:, :, pl.ds(column, HD)],
            qg.at[own_slot, :, pl.ds(multiple(own_piece * 64, 64), 64)],
            (task_of(index), head), me, q_send.at[index], q_recv,
        )
        return carry

    lax.fori_loop(0, 8, send_queries, 0)

    @pl.when(clean)
    def _():
        def send_keys(step, carry):
            chip = lax.rem(me // 2 + step, CHIPS)
            row = multiple(chip // 4 * STRIPE, STRIPE)
            column = multiple(chip // 2 % 2 * HD, HD)
            target = pl.ds(multiple(place * STRIPE, STRIPE), STRIPE)
            for kind, (source, there, send, recv) in enumerate(
                ((k_ref, kg, k_send, k_recv), (v_ref, vg, v_send, v_recv))
            ):
                push(
                    source.at[pl.ds(row, STRIPE), pl.ds(column, HD)],
                    there.at[target, pl.ds(0, HD)],
                    (2 * chip + kind, head), me, send.at[chip], recv,
                )
            return carry

        lax.fori_loop(0, CHIPS, send_keys, 0)

    def project(rows):
        return dot(rows, w_ref[...], CONTRACT_LAST).astype(BF16)

    part_row = lax.broadcasted_iota(jnp.int32, (SIDE, 64), 0)
    norm = n_ref[...].astype(F32) * (1.0 / SCALE)
    high = norm.astype(BF16).astype(F32)
    middle = (norm - high).astype(BF16).astype(F32)
    low = norm - high - middle
    for chunk in range(8):
        for h in range(2):
            cut = (slice(h, h + 1), slice(chunk * 64, (chunk + 1) * 64))
            rows = jnp.where(part_row == 0, high[cut], 0.0)
            rows = jnp.where(part_row == 1, middle[cut], rows)
            rows = jnp.where(part_row == 2, low[cut], rows)
            norms[chunk, h, :, 0:64] = rows

    def finish(chunk):
        rows = pl.ds(multiple(chunk * 64, 64), 64)
        for h in range(2):
            product = dl[chunk, h, 0:64, :].astype(F32) * o_ref[rows, h * HD:(h + 1) * HD].astype(F32)
            delta = jnp.sum(product.T, axis=0, keepdims=True).astype(BF16).astype(F32)
            extra = jnp.where(part_row == 3, delta, norms[chunk, h, :, 0:64])
            dl[chunk, h, 64:80, :] = jnp.concatenate(
                [extra, jnp.zeros((SIDE, 64), F32)], axis=1
            ).astype(BF16)

        def send(step, carry):
            index = lax.rem(me + step, 8)
            push(
                dl.at[chunk, index % 2],
                dg.at[own_slot, chunk, own_piece],
                (task_of(index), head), me, d_send.at[index], d_recv.at[chunk],
            )
            return carry

        lax.fori_loop(0, 8, send, 0)

    for number in range(2):
        fetches[number].wait()
    for number in range(2, 5):
        fetches[number].start()
    grad = project(g_ref[...])
    for h in range(2):
        dl[head, h, 0:64, :] = grad[:, h * HD:(h + 1) * HD]
    finish(head)

    kg[:, HD:] = pick(TASK_K, 0, 2)
    vg[:, HD:] = pick(TASK_K, 3, 3)
    dk_sum[...] = jnp.zeros_like(dk_sum)
    dv_sum[...] = jnp.zeros_like(dv_sum)
    in_group = lax.broadcasted_iota(jnp.int32, (32, HD), 0)

    def coarse_of(slot):
        return group + slot * (7 - 2 * group)

    def number_rows(index, carry):
        slot, chunk, half, pair = index // 32, index // 4 % 8, index // 2 % 2, index % 2
        pair = coarse_of(slot) * 32 + half * 16 + chunk * 2 + pair
        block = 2 * pair + jnp.where(in_group >= sizes[2 * pair], 1, 0)
        row = half * 64 + index % 2 * 32
        row_block[slot, chunk, pl.ds(multiple(row, 32), 32), :] = block
        row_block[slot, chunk, pl.ds(multiple(128 + row, 32), 32), :] = block + 1
        return carry

    lax.fori_loop(0, 64, number_rows, 0)
    row_lane = lax.broadcasted_iota(jnp.int32, (1, HD), 1)

    def number_keys(index, carry):
        blocks = []
        for half in range(2):
            pair = (index * 1024 + half * ROWS + x * STRIPE) // 32
            part = row_lane // 32
            size = jnp.where(
                part < 2,
                jnp.where(part == 0, sizes[2 * pair], sizes[2 * pair + 2]),
                jnp.where(part == 2, sizes[2 * pair + 4], sizes[2 * pair + 6]),
            )
            blocks.append(2 * (pair + part) + jnp.where(row_lane % 32 >= size, 1, 0))
        key_block[index] = jnp.concatenate(blocks, axis=1)
        return carry

    lax.fori_loop(0, 8, number_keys, 0)

    def query_owner(index):
        slot, kind, half = index // 4, index // 2 % 2, index % 2
        return kind * SHARDS + 2 * coarse_of(slot) + half

    def relay(there, recv):
        half = there.at[:, pl.ds(0, HD)]
        return pltpu.make_async_remote_copy(
            src_ref=half, dst_ref=half, send_sem=relay_send, recv_sem=recv,
            device_id=(sibling, head), device_id_type=MESH,
        )

    def attend(turn, carry):
        chunk = lax.rem(head + 8 + (turn + 1) // 2 * (1 - 2 * (turn % 2)), 8)

        @pl.when(turn == 0)
        def _():
            wait_bytes(qg, q_recv)
            for kind, (there, recv) in enumerate(((kg, k_recv), (vg, v_recv))):
                @pl.when(core == kind)
                def _():
                    wait_bytes(there.at[:, pl.ds(0, HD)], recv)
                    relay(there, recv).start()
            for kind, (there, recv) in enumerate(((vg, v_recv), (kg, k_recv))):
                @pl.when(core == kind)
                def _():
                    wait_bytes(there.at[:, pl.ds(0, HD)], recv)

        wait_bytes(dg.at[:, chunk], d_recv.at[chunk])
        dq_sum[...] = jnp.zeros_like(dq_sum)
        for slot in range(2):
            extras[slot] = side([dg[slot, chunk, piece, 64:80, :] for piece in range(4)])
            turned[slot, 0] = qg[slot, chunk].T
            turned[slot, 1] = dg[slot, chunk, :, 0:64, :].reshape(256, HD).T
        later = None
        for number in range(9):
            slot = 1 if number >= 4 else (number - group + 3) // 4
            pair = number - slot * (group + 1)
            keys = pl.ds(multiple(pair * 256, 256), 256)
            mask = None
            if number < 4 or number == 8:
                own = row_block[slot, chunk]
                mask = jnp.concatenate([own, own], axis=1) > key_block[pair]
            grads = dg[slot, chunk, :, 0:64, :].reshape(256, HD)
            dq, dk, dv = tile(
                qg[slot, chunk], grads, turned[slot, 0], turned[slot, 1], extras[slot],
                kg[keys, :], vg[keys, :], mask,
            )
            dk_sum[pair] += dk
            dv_sum[pair] += dv
            if number < 4:
                dq_sum[slot] += dq
            else:
                later = dq if later is None else later + dq
        first = (dq_sum[0] * SCALE).astype(BF16)
        second = ((dq_sum[1] + later) * SCALE).astype(BF16)
        for index in range(8):
            part = (first, second)[index // 4]
            dq_part[chunk, index] = part[index % 4 * 64:(index % 4 + 1) * 64]

        def send(step, inner):
            index = lax.rem(me + step, 8)
            push(
                dq_part.at[chunk, index],
                rq.at[x, chunk, :, pl.ds(multiple(which * HD, HD), HD)],
                (query_owner(index), head), me, dq_send.at[index], dq_recv,
            )
            return inner

        lax.fori_loop(0, 8, send, 0)
        return carry

    def attended(step):
        return step // 4 * (2 * step - 7) + step // 7

    def step(index, carry):
        for sub in range(2):
            for direction in range(2):
                source = landed.at[index, direction]
                ring(direction, index, sub, source).wait_recv()

                @pl.when(index < 5)
                def _():
                    ring(direction, lax.rem(index + 2, 7), sub, source).start()

        away = index // 2 + 1
        chunks = (lax.rem(head + 8 - away, 8), lax.rem(head + away, 8))
        units = (index % 2, 1 - index % 2)
        grad = project(landed[index].reshape(2 * UNIT, 4096))
        for direction in range(2):
            rows = pl.ds(multiple(units[direction] * UNIT, UNIT), UNIT)
            for h in range(2):
                dl[chunks[direction], h, rows, :] = grad[
                    direction * UNIT:(direction + 1) * UNIT, h * HD:(h + 1) * HD
                ]

        @pl.when(index % 2 == 1)
        def _():
            finish(chunks[0])

        @pl.when((index % 2 == 1) | (index == 6))
        def _():
            finish(chunks[1])

        lax.fori_loop(attended(index), attended(index + 1), attend, 0)
        return carry

    lax.fori_loop(0, 7, step, 0)

    def across(index):
        return pltpu.make_async_remote_copy(
            src_ref=to_sibling.at[index], dst_ref=from_sibling.at[index],
            send_sem=sibling_send.at[index], recv_sem=sibling_recv.at[index],
            device_id=(sibling, head), device_id_type=MESH,
        )

    def narrow(step, carry):
        index = lax.rem(me // 2 + step, 8)
        there = pl.ds(multiple((1 - core) * STRIPE, STRIPE), STRIPE)
        to_sibling[index, 0] = (dk_sum[index, :, there] * SCALE).T.astype(BF16)
        to_sibling[index, 1] = dv_sum[index, :, there].T.astype(BF16)
        across(index).start()
        return carry

    lax.fori_loop(0, 8, narrow, 0)

    def pass_on(step, carry):
        index = lax.rem(me // 2 + step, 8)
        here = pl.ds(multiple(core * STRIPE, STRIPE), STRIPE)
        across(index).wait_recv()
        key_part[index, 0] = (
            (dk_sum[index, :, here] * SCALE).T + from_sibling[index, 0].astype(F32)
        ).astype(BF16)
        key_part[index, 1] = (
            dv_sum[index, :, here].T + from_sibling[index, 1].astype(F32)
        ).astype(BF16)
        push(
            key_part.at[index],
            rk.at[y % 2, :, pl.ds(multiple(x * STRIPE, STRIPE), STRIPE), pl.ds(multiple(which * HD, HD), HD)],
            (SHARDS + 2 * index + core, head), me, part_send.at[index], part_recv,
        )
        return carry

    lax.fori_loop(0, 8, pass_on, 0)

    for number in range(2, 5):
        fetches[number].wait()

    @pl.when(me < SHARDS)
    def _():
        def number_own(index, carry):
            pair = place * 16 + index
            own_block[pl.ds(multiple(index * 32, 32), 32), :] = 2 * pair + jnp.where(
                in_group >= sizes[2 * pair], 1, 0
            )
            return carry

        lax.fori_loop(0, 16, number_own, 0)
        for part in range(4):
            rows = slice(part * STRIPE, (part + 1) * STRIPE)
            block = own_block[rows, :].astype(F32)
            mask = block == block.T
            for h in range(2):
                columns = slice(h * HD, (h + 1) * HD)
                own_q = q_own[2 * part:2 * part + 2, :, columns].reshape(STRIPE, HD)
                own_d = dl[2 * part:2 * part + 2, h, 0:64, :].reshape(STRIPE, HD)
                dq, dk, dv = tile(
                    own_q, own_d, own_q.T, own_d.T,
                    side([dl[2 * part + number, h, 64:80, :] for number in range(2)]),
                    jnp.concatenate([k_own[rows, columns], pick(STRIPE, 0, 2)], axis=1),
                    jnp.concatenate([v_own[rows, columns], pick(STRIPE, 3, 3)], axis=1),
                    mask,
                )
                dq_own[rows, columns] = dq * SCALE
                dk_out[rows, columns] = (dk * SCALE).T.astype(BF16)
                dv_out[rows, columns] = dv.T.astype(BF16)

    for index in range(7):
        for direction in range(2):
            for sub in range(2):
                ring(direction, index, sub, landed.at[index, direction]).wait_send()
    relay(kg, k_recv).wait_send()

    def settle(index, carry):
        @pl.when(task_of(index) != me)
        def _():
            wait_bytes(q_ref.at[:, :, pl.ds(0, HD)], q_send.at[index])
            wait_bytes(dl.at[:, 0], d_send.at[index])
        return carry

    lax.fori_loop(0, 8, settle, 0)

    @pl.when(clean)
    def _():
        def settle_keys(chip, carry):
            for kind, (source, send) in enumerate(((k_ref, k_send), (v_ref, v_send))):
                @pl.when(2 * chip + kind != me)
                def _():
                    wait_bytes(source.at[pl.ds(0, STRIPE), pl.ds(0, HD)], send.at[chip])
            return carry

        lax.fori_loop(0, CHIPS, settle_keys, 0)

    wait_bytes(rq, dq_recv)

    def summed_queries():
        parts = [rq[stripe].reshape(ROWS, 256).astype(F32) for stripe in range(4)]
        return (parts[0] + parts[1]) + (parts[2] + parts[3])

    @pl.when(me < SHARDS)
    def _():
        dq_out[...] = (summed_queries() + dq_own[...]).astype(BF16)

    @pl.when(clean)
    def _():
        dq_out[...] = summed_queries().astype(BF16)
        wait_bytes(rk, part_recv)
        dk_out[...] = (rk[0, 0].astype(F32) + rk[1, 0].astype(F32)).astype(BF16)
        dv_out[...] = (rk[0, 1].astype(F32) + rk[1, 1].astype(F32)).astype(BF16)

    def settle_last(index, carry):
        across(index).wait_send()

        @pl.when(query_owner(index) != me)
        def _():
            wait_bytes(dq_part.at[:, index], dq_send.at[index])

        @pl.when(SHARDS + 2 * index + core != me)
        def _():
            wait_bytes(key_part.at[index], part_send.at[index])
        return carry

    lax.fori_loop(0, 8, settle_last, 0)


ANY = pl.BlockSpec(memory_space=pl.ANY)
VMEM = pl.BlockSpec(memory_space=pltpu.VMEM)
SMEM = pl.BlockSpec(memory_space=pltpu.SMEM)
DMA = pltpu.SemaphoreType.DMA
LIMIT = 56 * 1024 * 1024


def hand_on_kernel(*refs):
    for source, target in zip(refs[:3], refs[3:]):
        target[...] = source[...]


def hand_on(results):
    return pl.pallas_call(
        hand_on_kernel,
        name="hand_on",
        out_shape=(jax.ShapeDtypeStruct((ROWS, 256), BF16),) * 3,
        in_specs=[VMEM] * 3,
        out_specs=(VMEM,) * 3,
        compiler_params=pltpu.CompilerParams(vmem_limit_bytes=LIMIT),
    )(*results)


def shards(queries, keys, values, attn_out, out_grad, out_weight, log_norm, block_sizes):
    results = pl.pallas_call(
        layer_kernel,
        name="layer",
        out_shape=(jax.ShapeDtypeStruct((ROWS, 256), BF16),) * 3,
        in_specs=[SMEM] + [ANY] * 5 + [VMEM] * 2,
        out_specs=(VMEM,) * 3,
        scratch_shapes=[
            pltpu.VMEM((64, 4096), BF16),
            pltpu.VMEM((256, 4096), BF16),
            pltpu.VMEM((8, 64, 256), BF16),
            pltpu.VMEM((ROWS, 256), BF16),
            pltpu.VMEM((ROWS, 256), BF16),
            pltpu.VMEM((7, 2, UNIT, 4096), BF16),
            pltpu.VMEM((2, 8, 256, HD), BF16),
            pltpu.VMEM((2, 8, 4, 64 + SIDE, HD), BF16),
            pltpu.VMEM((TASK_K, 256), BF16),
            pltpu.VMEM((TASK_K, 256), BF16),
            pltpu.VMEM((8, 2, 64 + SIDE, HD), BF16),
            pltpu.VMEM((8, 2, SIDE, HD), F32),
            pltpu.VMEM((2, 256, HD), BF16),
            pltpu.VMEM((2, 2, HD, 256), BF16),
            pltpu.VMEM((2, 256, HD), F32),
            pltpu.VMEM((8, HD, 256), F32),
            pltpu.VMEM((8, HD, 256), F32),
            pltpu.VMEM((2, 8, 256, HD), jnp.int32),
            pltpu.VMEM((8, 1, 256), jnp.int32),
            pltpu.VMEM((ROWS, HD), jnp.int32),
            pltpu.VMEM((ROWS, 256), F32),
            pltpu.VMEM((8, 8, 64, HD), BF16),
            pltpu.VMEM((8, 2, STRIPE, HD), BF16),
            pltpu.VMEM((8, 2, STRIPE, HD), BF16),
            pltpu.VMEM((8, 2, STRIPE, HD), BF16),
            pltpu.VMEM((4, 8, 64, 256), BF16),
            pltpu.VMEM((2, 2, ROWS, 256), BF16),
            DMA((2, 7, 2)), DMA((2, 7, 2)), DMA((8,)), DMA((CHIPS,)), DMA((CHIPS,)), DMA((8,)),
            DMA, DMA, DMA, DMA((8,)),
            DMA((8,)), DMA, DMA((8,)), DMA((8,)), DMA((8,)), DMA, DMA, DMA((5,)),
        ],
        compiler_params=pltpu.CompilerParams(
            collective_id=0, has_side_effects=True, vmem_limit_bytes=LIMIT
        ),
    )(
        block_sizes, queries.reshape(8, 64, 256), keys, values, out_grad, out_weight, attn_out,
        log_norm.T,
    )
    return hand_on(results)


def solution(mesh):
    in_specs = (
        P("seq", "head"),
        P("seq", "head"),
        P("seq", "head"),
        P("seq", "head"),
        P(("seq", "head"), None),
        P("head", None),
        P("seq", "head"),
        P(),
    )
    out_specs = (P("seq", "head"), P("seq", "head"), P("seq", "head"))
    return jax.shard_map(shards, mesh=mesh, in_specs=in_specs, out_specs=out_specs, check_vma=False)
```

```python
import functools
import math

import jax
import jax.numpy as jnp
from jax import lax
from jax.experimental import pallas as pl
from jax.experimental.pallas import tpu as pltpu
from jax.sharding import PartitionSpec as P

HD = 128
UNIT = 32
HALF_UNIT = 16
SIDE = 16
ROWS = 512
STRIPE = 128
TASK_K = 2048
PEERS = 32
SHARDS = 16
CHIPS = 16
SCALE = HD ** -0.5
MESH = pl.DeviceIdType.MESH
F32 = jnp.float32
BF16 = jnp.bfloat16
CONTRACT = (((1,), (0,)), ((), ()))
CONTRACT_LAST = (((1,), (1,)), ((), ()))
CONTRACT_FIRST = (((0,), (0,)), ((), ()))


def where_am_i():
    seq = lax.axis_index("seq")
    return seq, seq // 8, (seq // 2) % 4, seq % 2


def multiple(value, of):
    return pl.multiple_of(value, of)


def push(here, there, device, me, send_sem, recv_sem):
    seq, head = device

    @pl.when(seq == me)
    def _():
        pltpu.make_async_copy(here, there, recv_sem).start()

    @pl.when(seq != me)
    def _():
        pltpu.make_async_remote_copy(
            src_ref=here, dst_ref=there, send_sem=send_sem, recv_sem=recv_sem,
            device_id=(seq, head), device_id_type=MESH,
        ).start()


def wait_bytes(ref, sem):
    pltpu.make_async_copy(ref, ref, sem).wait()


def dot(a, b, dims):
    return lax.dot_general(a, b, dims, preferred_element_type=F32)


def tile(q, d, turned_q, turned_d, extra, keys, values, mask):
    score = dot(jnp.concatenate([q, extra], axis=1), keys, CONTRACT_LAST)
    probs = jnp.exp2(score * (SCALE * math.log2(math.e)))
    if mask is not None:
        probs = jnp.where(mask, probs, 0.0)
    grad = (probs * dot(jnp.concatenate([d, extra], axis=1), values, CONTRACT_LAST)).astype(BF16)
    dq = dot(grad, keys[:, :HD], CONTRACT)
    dk = dot(turned_q, grad, CONTRACT)
    dv = dot(turned_d, probs.astype(BF16), CONTRACT)
    return dq, dk, dv


def pick(rows, first, last):
    lane = lax.broadcasted_iota(jnp.int32, (rows, HD), 1)
    part = lane % SIDE
    return jnp.where((lane < 4 * SIDE) & (part >= first) & (part <= last), -1.0, 0.0).astype(BF16)


def side(pieces):
    stacked = jnp.concatenate([piece.astype(F32) for piece in pieces], axis=0)
    filler = jnp.zeros((HD - stacked.shape[0], HD), F32)
    turned = jnp.concatenate([stacked, filler], axis=0).T[:64]
    lane = lax.broadcasted_iota(jnp.int32, (64, HD), 1)
    return jnp.concatenate(
        [jnp.where(lane // SIDE == number, turned, 0.0) for number in range(len(pieces))], axis=0
    ).astype(BF16)


def layer_kernel(
    sizes, q_ref, k_ref, v_ref, g_hbm, w_hbm, o_ref, n_ref,
    dq_out, dk_out, dv_out,
    g_ref, w_ref, q_own, k_own, v_own,
    landed, qg, dg, kg, vg, dl, norms, extras, turned,
    dq_sum, dk_sum, dv_sum, row_block, key_block, own_block, dq_own,
    dq_part, to_sibling, from_sibling, key_part, rq, rk,
    ring_send, ring_recv, q_send, k_send, v_send, d_send, q_recv, k_recv, v_recv, d_recv,
    dq_send, dq_recv, sibling_send, sibling_recv, part_send, part_recv, relay_send, fetch,
):
    me, x, y, core = where_am_i()
    head = lax.axis_index("head")
    right, left = lax.rem(head + 1, 8), lax.rem(head + 7, 8)
    place = me % SHARDS
    clean = me >= SHARDS
    own_slot = x % 2
    own_group = y + own_slot * (3 - 2 * y)
    own_piece = (x // 2) * 2 + core
    group = core * 2 + y % 2
    which = y // 2
    sibling = me + 1 - 2 * core

    fetches = [
        pltpu.make_async_copy(source, target, fetch.at[number])
        for number, (source, target) in enumerate(
            ((g_hbm, g_ref), (w_hbm, w_ref), (q_ref, q_own), (k_ref, k_own), (v_ref, v_own))
        )
    ]
    for number in range(2):
        fetches[number].start()

    barrier = pltpu.get_barrier_semaphore()

    def greet(step, carry):
        pl.semaphore_signal(
            barrier, inc=1, device_id=(lax.rem(me + step, PEERS), head), device_id_type=MESH
        )
        return carry

    lax.fori_loop(1, PEERS, greet, 0)
    for neighbour in (left, right):
        pl.semaphore_signal(barrier, inc=1, device_id=(me, neighbour), device_id_type=MESH)
    pl.semaphore_wait(barrier, PEERS + 1)

    def ring(direction, index, sub, source):
        rows = pl.ds(sub * HALF_UNIT, HALF_UNIT)
        return pltpu.make_async_remote_copy(
            src_ref=source.at[rows],
            dst_ref=landed.at[index, direction, rows],
            send_sem=ring_send.at[direction, index, sub],
            recv_sem=ring_recv.at[direction, index, sub],
            device_id=(me, (right, left)[direction]),
            device_id_type=MESH,
        )

    for index in range(2):
        for sub in range(2):
            for direction in range(2):
                unit = index if direction == 0 else 1 - index
                ring(direction, index, sub, g_hbm.at[pl.ds(unit * UNIT, UNIT)]).start()

    def task_of(index):
        stripe, part = index // 2, index % 2
        return (stripe * 4 + 2 * part + own_group % 2) * 2 + own_group // 2

    def send_queries(step, carry):
        index = lax.rem(me + step, 8)
        column = multiple(index % 2 * HD, HD)
        push(
            q_ref.at[:, :, pl.ds(column, HD)],
            qg.at[own_slot, :, pl.ds(multiple(own_piece * 64, 64), 64)],
            (task_of(index), head), me, q_send.at[index], q_recv,
        )
        return carry

    lax.fori_loop(0, 8, send_queries, 0)

    @pl.when(clean)
    def _():
        def send_keys(step, carry):
            chip = lax.rem(me // 2 + step, CHIPS)
            row = multiple(chip // 4 * STRIPE, STRIPE)
            column = multiple(chip // 2 % 2 * HD, HD)
            target = pl.ds(multiple(place * STRIPE, STRIPE), STRIPE)
            for kind, (source, there, send, recv) in enumerate(
                ((k_ref, kg, k_send, k_recv), (v_ref, vg, v_send, v_recv))
            ):
                push(
                    source.at[pl.ds(row, STRIPE), pl.ds(column, HD)],
                    there.at[target, pl.ds(0, HD)],
                    (2 * chip + kind, head), me, send.at[chip], recv,
                )
            return carry

        lax.fori_loop(0, CHIPS, send_keys, 0)

    def project(rows):
        return dot(rows, w_ref[...], CONTRACT_LAST).astype(BF16)

    part_row = lax.broadcasted_iota(jnp.int32, (SIDE, 64), 0)
    norm = n_ref[...].astype(F32) * (1.0 / SCALE)
    high = norm.astype(BF16).astype(F32)
    middle = (norm - high).astype(BF16).astype(F32)
    low = norm - high - middle
    for chunk in range(8):
        for h in range(2):
            cut = (slice(h, h + 1), slice(chunk * 64, (chunk + 1) * 64))
            rows = jnp.where(part_row == 0, high[cut], 0.0)
            rows = jnp.where(part_row == 1, middle[cut], rows)
            rows = jnp.where(part_row == 2, low[cut], rows)
            norms[chunk, h, :, 0:64] = rows

    def finish(chunk):
        rows = pl.ds(multiple(chunk * 64, 64), 64)
        for h in range(2):
            product = dl[chunk, h, 0:64, :].astype(F32) * o_ref[rows, h * HD:(h + 1) * HD].astype(F32)
            delta = jnp.sum(product.T, axis=0, keepdims=True).astype(BF16).astype(F32)
            extra = jnp.where(part_row == 3, delta, norms[chunk, h, :, 0:64])
            dl[chunk, h, 64:80, :] = jnp.concatenate(
                [extra, jnp.zeros((SIDE, 64), F32)], axis=1
            ).astype(BF16)

        def send(step, carry):
            index = lax.rem(me + step, 8)
            push(
                dl.at[chunk, index % 2],
                dg.at[own_slot, chunk, own_piece],
                (task_of(index), head), me, d_send.at[index], d_recv.at[chunk],
            )
            return carry

        lax.fori_loop(0, 8, send, 0)

    for number in range(2):
        fetches[number].wait()
    for number in range(2, 5):
        fetches[number].start()
    grad = project(g_ref[...])
    for h in range(2):
        dl[head, h, 0:64, :] = grad[:, h * HD:(h + 1) * HD]
    finish(head)

    kg[:, HD:] = pick(TASK_K, 0, 2)
    vg[:, HD:] = pick(TASK_K, 3, 3)
    dk_sum[...] = jnp.zeros_like(dk_sum)
    dv_sum[...] = jnp.zeros_like(dv_sum)
    in_group = lax.broadcasted_iota(jnp.int32, (32, HD), 0)

    def coarse_of(slot):
        return group + slot * (7 - 2 * group)

    def number_rows(index, carry):
        slot, chunk, half, pair = index // 32, index // 4 % 8, index // 2 % 2, index % 2
        pair = coarse_of(slot) * 32 + half * 16 + chunk * 2 + pair
        block = 2 * pair + jnp.where(in_group >= sizes[2 * pair], 1, 0)
        row = half * 64 + index % 2 * 32
        row_block[slot, chunk, pl.ds(multiple(row, 32), 32), :] = block
        row_block[slot, chunk, pl.ds(multiple(128 + row, 32), 32), :] = block + 1
        return carry

    lax.fori_loop(0, 64, number_rows, 0)
    row_lane = lax.broadcasted_iota(jnp.int32, (1, HD), 1)

    def number_keys(index, carry):
        blocks = []
        for half in range(2):
            pair = (index * 1024 + half * ROWS + x * STRIPE) // 32
            part = row_lane // 32
            size = jnp.where(
                part < 2,
                jnp.where(part == 0, sizes[2 * pair], sizes[2 * pair + 2]),
                jnp.where(part == 2, sizes[2 * pair + 4], sizes[2 * pair + 6]),
            )
            blocks.append(2 * (pair + part) + jnp.where(row_lane % 32 >= size, 1, 0))
        key_block[index] = jnp.concatenate(blocks, axis=1)
        return carry

    lax.fori_loop(0, 8, number_keys, 0)

    def query_owner(index):
        slot, kind, half = index // 4, index // 2 % 2, index % 2
        return kind * SHARDS + 2 * coarse_of(slot) + half

    def relay(there, recv):
        half = there.at[:, pl.ds(0, HD)]
        return pltpu.make_async_remote_copy(
            src_ref=half, dst_ref=half, send_sem=relay_send, recv_sem=recv,
            device_id=(sibling, head), device_id_type=MESH,
        )

    def attend(turn, carry):
        chunk = lax.rem(head + 8 + (turn + 1) // 2 * (1 - 2 * (turn % 2)), 8)

        @pl.when(turn == 0)
        def _():
            wait_bytes(qg, q_recv)
            for kind, (there, recv) in enumerate(((kg, k_recv), (vg, v_recv))):
                @pl.when(core == kind)
                def _():
                    wait_bytes(there.at[:, pl.ds(0, HD)], recv)
                    relay(there, recv).start()
            for kind, (there, recv) in enumerate(((vg, v_recv), (kg, k_recv))):
                @pl.when(core == kind)
                def _():
                    wait_bytes(there.at[:, pl.ds(0, HD)], recv)

        wait_bytes(dg.at[:, chunk], d_recv.at[chunk])
        dq_sum[...] = jnp.zeros_like(dq_sum)
        for slot in range(2):
            extras[slot] = side([dg[slot, chunk, piece, 64:80, :] for piece in range(4)])
            turned[slot, 0] = qg[slot, chunk].T
            turned[slot, 1] = dg[slot, chunk, :, 0:64, :].reshape(256, HD).T
        later = None
        for number, wide in ((0, 1), (1, 1), (2, 1), (3, 1), (4, 2), (6, 2), (8, 1)):
            slot = 1 if number >= 4 else (number - group + 3) // 4
            pair = number - slot * (group + 1)
            keys = pl.ds(multiple(pair * 256, 256), wide * 256)
            mask = None
            if number < 4 or number == 8:
                own = row_block[slot, chunk]
                mask = jnp.concatenate([own, own], axis=1) > key_block[pair]
            grads = dg[slot, chunk, :, 0:64, :].reshape(256, HD)
            dq, dk, dv = tile(
                qg[slot, chunk], grads, turned[slot, 0], turned[slot, 1], extras[slot],
                kg[keys, :], vg[keys, :], mask,
            )
            for step in range(wide):
                dk_sum[pair + step] += dk[:, step * 256:(step + 1) * 256]
                dv_sum[pair + step] += dv[:, step * 256:(step + 1) * 256]
            if number < 4:
                dq_sum[slot] += dq
            else:
                later = dq if later is None else later + dq
        first = (dq_sum[0] * SCALE).astype(BF16)
        second = ((dq_sum[1] + later) * SCALE).astype(BF16)
        for index in range(8):
            part = (first, second)[index // 4]
            dq_part[chunk, index] = part[index % 4 * 64:(index % 4 + 1) * 64]

        def send(step, inner):
            index = lax.rem(me + step, 8)
            push(
                dq_part.at[chunk, index],
                rq.at[x, chunk, :, pl.ds(multiple(which * HD, HD), HD)],
                (query_owner(index), head), me, dq_send.at[index], dq_recv,
            )
            return inner

        lax.fori_loop(0, 8, send, 0)
        return carry

    def attended(step):
        return step // 4 * (2 * step - 7) + step // 7

    def step(index, carry):
        for sub in range(2):
            for direction in range(2):
                source = landed.at[index, direction]
                ring(direction, index, sub, source).wait_recv()

                @pl.when(index < 5)
                def _():
                    ring(direction, lax.rem(index + 2, 7), sub, source).start()

        away = index // 2 + 1
        chunks = (lax.rem(head + 8 - away, 8), lax.rem(head + away, 8))
        units = (index % 2, 1 - index % 2)
        grad = project(landed[index].reshape(2 * UNIT, 4096))
        for direction in range(2):
            rows = pl.ds(multiple(units[direction] * UNIT, UNIT), UNIT)
            for h in range(2):
                dl[chunks[direction], h, rows, :] = grad[
                    direction * UNIT:(direction + 1) * UNIT, h * HD:(h + 1) * HD
                ]

        @pl.when(index % 2 == 1)
        def _():
            finish(chunks[0])

        @pl.when((index % 2 == 1) | (index == 6))
        def _():
            finish(chunks[1])

        lax.fori_loop(attended(index), attended(index + 1), attend, 0)
        return carry

    lax.fori_loop(0, 7, step, 0)

    def across(index):
        return pltpu.make_async_remote_copy(
            src_ref=to_sibling.at[index], dst_ref=from_sibling.at[index],
            send_sem=sibling_send.at[index], recv_sem=sibling_recv.at[index],
            device_id=(sibling, head), device_id_type=MESH,
        )

    def narrow(step, carry):
        index = lax.rem(me // 2 + step, 8)
        there = pl.ds(multiple((1 - core) * STRIPE, STRIPE), STRIPE)
        to_sibling[index, 0] = (dk_sum[index, :, there] * SCALE).T.astype(BF16)
        to_sibling[index, 1] = dv_sum[index, :, there].T.astype(BF16)
        across(index).start()
        return carry

    def pass_on(step, carry):
        index = lax.rem(me // 2 + step, 8)
        here = pl.ds(multiple(core * STRIPE, STRIPE), STRIPE)
        across(index).wait_recv()
        key_part[index, 0] = (
            (dk_sum[index, :, here] * SCALE).T + from_sibling[index, 0].astype(F32)
        ).astype(BF16)
        key_part[index, 1] = (
            dv_sum[index, :, here].T + from_sibling[index, 1].astype(F32)
        ).astype(BF16)
        push(
            key_part.at[index],
            rk.at[y % 2, :, pl.ds(multiple(x * STRIPE, STRIPE), STRIPE), pl.ds(multiple(which * HD, HD), HD)],
            (SHARDS + 2 * index + core, head), me, part_send.at[index], part_recv,
        )
        return carry

    def both(step, carry):
        narrow(step + 2, carry)
        return pass_on(step, carry)

    lax.fori_loop(0, 2, narrow, 0)
    lax.fori_loop(0, 6, both, 0)
    lax.fori_loop(6, 8, pass_on, 0)

    for number in range(2, 5):
        fetches[number].wait()

    @pl.when(me < SHARDS)
    def _():
        def number_own(index, carry):
            pair = place * 16 + index
            own_block[pl.ds(multiple(index * 32, 32), 32), :] = 2 * pair + jnp.where(
                in_group >= sizes[2 * pair], 1, 0
            )
            return carry

        lax.fori_loop(0, 16, number_own, 0)
        for part in range(4):
            rows = slice(part * STRIPE, (part + 1) * STRIPE)
            block = own_block[rows, :].astype(F32)
            mask = block == block.T
            for h in range(2):
                columns = slice(h * HD, (h + 1) * HD)
                own_q = q_own[2 * part:2 * part + 2, :, columns].reshape(STRIPE, HD)
                own_d = dl[2 * part:2 * part + 2, h, 0:64, :].reshape(STRIPE, HD)
                dq, dk, dv = tile(
                    own_q, own_d, own_q.T, own_d.T,
                    side([dl[2 * part + number, h, 64:80, :] for number in range(2)]),
                    jnp.concatenate([k_own[rows, columns], pick(STRIPE, 0, 2)], axis=1),
                    jnp.concatenate([v_own[rows, columns], pick(STRIPE, 3, 3)], axis=1),
                    mask,
                )
                dq_own[rows, columns] = dq * SCALE
                dk_out[rows, columns] = (dk * SCALE).T.astype(BF16)
                dv_out[rows, columns] = dv.T.astype(BF16)

    for index in range(7):
        for direction in range(2):
            for sub in range(2):
                ring(direction, index, sub, landed.at[index, direction]).wait_send()
    relay(kg, k_recv).wait_send()

    def settle(index, carry):
        @pl.when(task_of(index) != me)
        def _():
            wait_bytes(q_ref.at[:, :, pl.ds(0, HD)], q_send.at[index])
            wait_bytes(dl.at[:, 0], d_send.at[index])
        return carry

    lax.fori_loop(0, 8, settle, 0)

    @pl.when(clean)
    def _():
        def settle_keys(chip, carry):
            for kind, (source, send) in enumerate(((k_ref, k_send), (v_ref, v_send))):
                @pl.when(2 * chip + kind != me)
                def _():
                    wait_bytes(source.at[pl.ds(0, STRIPE), pl.ds(0, HD)], send.at[chip])
            return carry

        lax.fori_loop(0, CHIPS, settle_keys, 0)

    wait_bytes(rq, dq_recv)

    def summed_queries():
        parts = [rq[stripe].reshape(ROWS, 256).astype(F32) for stripe in range(4)]
        return (parts[0] + parts[1]) + (parts[2] + parts[3])

    @pl.when(me < SHARDS)
    def _():
        dq_out[...] = (summed_queries() + dq_own[...]).astype(BF16)

    @pl.when(clean)
    def _():
        dq_out[...] = summed_queries().astype(BF16)
        wait_bytes(rk, part_recv)
        dk_out[...] = (rk[0, 0].astype(F32) + rk[1, 0].astype(F32)).astype(BF16)
        dv_out[...] = (rk[0, 1].astype(F32) + rk[1, 1].astype(F32)).astype(BF16)

    def settle_last(index, carry):
        across(index).wait_send()

        @pl.when(query_owner(index) != me)
        def _():
            wait_bytes(dq_part.at[:, index], dq_send.at[index])

        @pl.when(SHARDS + 2 * index + core != me)
        def _():
            wait_bytes(key_part.at[index], part_send.at[index])
        return carry

    lax.fori_loop(0, 8, settle_last, 0)


ANY = pl.BlockSpec(memory_space=pl.ANY)
VMEM = pl.BlockSpec(memory_space=pltpu.VMEM)
SMEM = pl.BlockSpec(memory_space=pltpu.SMEM)
DMA = pltpu.SemaphoreType.DMA
LIMIT = 56 * 1024 * 1024


def hand_on_kernel(*refs):
    for source, target in zip(refs[:3], refs[3:]):
        target[...] = source[...]


def hand_on(results):
    return pl.pallas_call(
        hand_on_kernel,
        name="hand_on",
        out_shape=(jax.ShapeDtypeStruct((ROWS, 256), BF16),) * 3,
        in_specs=[VMEM] * 3,
        out_specs=(VMEM,) * 3,
        compiler_params=pltpu.CompilerParams(vmem_limit_bytes=LIMIT),
    )(*results)


def shards(queries, keys, values, attn_out, out_grad, out_weight, log_norm, block_sizes):
    results = pl.pallas_call(
        layer_kernel,
        name="layer",
        out_shape=(jax.ShapeDtypeStruct((ROWS, 256), BF16),) * 3,
        in_specs=[SMEM] + [ANY] * 5 + [VMEM] * 2,
        out_specs=(VMEM,) * 3,
        scratch_shapes=[
            pltpu.VMEM((64, 4096), BF16),
            pltpu.VMEM((256, 4096), BF16),
            pltpu.VMEM((8, 64, 256), BF16),
            pltpu.VMEM((ROWS, 256), BF16),
            pltpu.VMEM((ROWS, 256), BF16),
            pltpu.VMEM((7, 2, UNIT, 4096), BF16),
            pltpu.VMEM((2, 8, 256, HD), BF16),
            pltpu.VMEM((2, 8, 4, 64 + SIDE, HD), BF16),
            pltpu.VMEM((TASK_K, 256), BF16),
            pltpu.VMEM((TASK_K, 256), BF16),
            pltpu.VMEM((8, 2, 64 + SIDE, HD), BF16),
            pltpu.VMEM((8, 2, SIDE, HD), F32),
            pltpu.VMEM((2, 256, HD), BF16),
            pltpu.VMEM((2, 2, HD, 256), BF16),
            pltpu.VMEM((2, 256, HD), F32),
            pltpu.VMEM((8, HD, 256), F32),
            pltpu.VMEM((8, HD, 256), F32),
            pltpu.VMEM((2, 8, 256, HD), jnp.int32),
            pltpu.VMEM((8, 1, 256), jnp.int32),
            pltpu.VMEM((ROWS, HD), jnp.int32),
            pltpu.VMEM((ROWS, 256), F32),
            pltpu.VMEM((8, 8, 64, HD), BF16),
            pltpu.VMEM((8, 2, STRIPE, HD), BF16),
            pltpu.VMEM((8, 2, STRIPE, HD), BF16),
            pltpu.VMEM((8, 2, STRIPE, HD), BF16),
            pltpu.VMEM((4, 8, 64, 256), BF16),
            pltpu.VMEM((2, 2, ROWS, 256), BF16),
            DMA((2, 7, 2)), DMA((2, 7, 2)), DMA((8,)), DMA((CHIPS,)), DMA((CHIPS,)), DMA((8,)),
            DMA, DMA, DMA, DMA((8,)),
            DMA((8,)), DMA, DMA((8,)), DMA((8,)), DMA((8,)), DMA, DMA, DMA((5,)),
        ],
        compiler_params=pltpu.CompilerParams(
            collective_id=0, has_side_effects=True, vmem_limit_bytes=LIMIT
        ),
    )(
        block_sizes, queries.reshape(8, 64, 256), keys, values, out_grad, out_weight, attn_out,
        log_norm.T,
    )
    return hand_on(results)


def solution(mesh):
    in_specs = (
        P("seq", "head"),
        P("seq", "head"),
        P("seq", "head"),
        P("seq", "head"),
        P(("seq", "head"), None),
        P("head", None),
        P("seq", "head"),
        P(),
    )
    out_specs = (P("seq", "head"), P("seq", "head"), P("seq", "head"))
    return jax.shard_map(shards, mesh=mesh, in_specs=in_specs, out_specs=out_specs, check_vma=False)
```

```python
import functools
import math

import jax
import jax.numpy as jnp
from jax import lax
from jax.experimental import pallas as pl
from jax.experimental.pallas import tpu as pltpu
from jax.sharding import PartitionSpec as P

HD = 128
UNIT = 32
HALF_UNIT = 16
SIDE = 16
ROWS = 512
STRIPE = 128
TASK_K = 2048
PEERS = 32
SHARDS = 16
CHIPS = 16
SCALE = HD ** -0.5
MESH = pl.DeviceIdType.MESH
F32 = jnp.float32
BF16 = jnp.bfloat16
CONTRACT = (((1,), (0,)), ((), ()))
CONTRACT_LAST = (((1,), (1,)), ((), ()))
CONTRACT_FIRST = (((0,), (0,)), ((), ()))


def where_am_i():
    seq = lax.axis_index("seq")
    return seq, seq // 8, (seq // 2) % 4, seq % 2


def multiple(value, of):
    return pl.multiple_of(value, of)


def push(here, there, device, me, send_sem, recv_sem):
    seq, head = device

    @pl.when(seq == me)
    def _():
        pltpu.make_async_copy(here, there, recv_sem).start()

    @pl.when(seq != me)
    def _():
        pltpu.make_async_remote_copy(
            src_ref=here, dst_ref=there, send_sem=send_sem, recv_sem=recv_sem,
            device_id=(seq, head), device_id_type=MESH,
        ).start()


def wait_bytes(ref, sem):
    pltpu.make_async_copy(ref, ref, sem).wait()


def dot(a, b, dims):
    return lax.dot_general(a, b, dims, preferred_element_type=F32)


def tile(q, d, turned_q, turned_d, extra, keys, values, mask):
    score = dot(jnp.concatenate([q, extra], axis=1), keys, CONTRACT_LAST)
    probs = jnp.exp2(score * (SCALE * math.log2(math.e)))
    if mask is not None:
        probs = jnp.where(mask, probs, 0.0)
    grad = (probs * dot(jnp.concatenate([d, extra], axis=1), values, CONTRACT_LAST)).astype(BF16)
    dq = dot(grad, keys[:, :HD], CONTRACT)
    dk = dot(turned_q, grad, CONTRACT)
    dv = dot(turned_d, probs.astype(BF16), CONTRACT)
    return dq, dk, dv


def pick(rows, first, last):
    lane = lax.broadcasted_iota(jnp.int32, (rows, HD), 1)
    part = lane % SIDE
    return jnp.where((lane < 4 * SIDE) & (part >= first) & (part <= last), -1.0, 0.0).astype(BF16)


def side(pieces):
    stacked = jnp.concatenate([piece.astype(F32) for piece in pieces], axis=0)
    filler = jnp.zeros((HD - stacked.shape[0], HD), F32)
    turned = jnp.concatenate([stacked, filler], axis=0).T[:64]
    lane = lax.broadcasted_iota(jnp.int32, (64, HD), 1)
    return jnp.concatenate(
        [jnp.where(lane // SIDE == number, turned, 0.0) for number in range(len(pieces))], axis=0
    ).astype(BF16)


def layer_kernel(
    sizes, q_ref, k_ref, v_ref, g_hbm, w_hbm, o_ref, n_ref,
    dq_out, dk_out, dv_out,
    g_ref, w_ref, q_own, k_own, v_own,
    landed, qg, dg, kg, vg, dl, norms, extras, turned,
    dq_sum, dk_sum, dv_sum, row_block, key_block, own_block, dq_own,
    dq_part, to_sibling, from_sibling, key_part, rq, rk,
    ring_send, ring_recv, q_send, k_send, v_send, d_send, q_recv, k_recv, v_recv, d_recv,
    dq_send, dq_recv, sibling_send, sibling_recv, part_send, part_recv, relay_send, fetch,
):
    me, x, y, core = where_am_i()
    head = lax.axis_index("head")
    right, left = lax.rem(head + 1, 8), lax.rem(head + 7, 8)
    place = me % SHARDS
    clean = me >= SHARDS
    own_slot = x % 2
    own_group = y + own_slot * (3 - 2 * y)
    own_piece = (x // 2) * 2 + core
    group = core * 2 + y % 2
    which = y // 2
    sibling = me + 1 - 2 * core

    fetches = [
        pltpu.make_async_copy(source, target, fetch.at[number])
        for number, (source, target) in enumerate(
            ((g_hbm, g_ref), (w_hbm, w_ref), (q_ref, q_own), (k_ref, k_own), (v_ref, v_own))
        )
    ]
    for number in range(2):
        fetches[number].start()

    barrier = pltpu.get_barrier_semaphore()

    def greet(step, carry):
        pl.semaphore_signal(
            barrier, inc=1, device_id=(lax.rem(me + step, PEERS), head), device_id_type=MESH
        )
        return carry

    lax.fori_loop(1, PEERS, greet, 0)
    for neighbour in (left, right):
        pl.semaphore_signal(barrier, inc=1, device_id=(me, neighbour), device_id_type=MESH)
    pl.semaphore_wait(barrier, PEERS + 1)

    def ring(direction, index, sub, source):
        rows = pl.ds(sub * HALF_UNIT, HALF_UNIT)
        return pltpu.make_async_remote_copy(
            src_ref=source.at[rows],
            dst_ref=landed.at[index, direction, rows],
            send_sem=ring_send.at[direction, index, sub],
            recv_sem=ring_recv.at[direction, index, sub],
            device_id=(me, (right, left)[direction]),
            device_id_type=MESH,
        )

    for index in range(2):
        for sub in range(2):
            for direction in range(2):
                unit = index if direction == 0 else 1 - index
                ring(direction, index, sub, g_hbm.at[pl.ds(unit * UNIT, UNIT)]).start()

    def task_of(index):
        stripe, part = index // 2, index % 2
        return (stripe * 4 + 2 * part + own_group % 2) * 2 + own_group // 2

    def send_queries(step, carry):
        index = lax.rem(me + step, 8)
        column = multiple(index % 2 * HD, HD)
        push(
            q_ref.at[:, :, pl.ds(column, HD)],
            qg.at[own_slot, :, pl.ds(multiple(own_piece * 64, 64), 64)],
            (task_of(index), head), me, q_send.at[index], q_recv,
        )
        return carry

    lax.fori_loop(0, 8, send_queries, 0)

    @pl.when(clean)
    def _():
        def send_keys(step, carry):
            chip = lax.rem(me // 2 + step, CHIPS)
            row = multiple(chip // 4 * STRIPE, STRIPE)
            column = multiple(chip // 2 % 2 * HD, HD)
            target = pl.ds(multiple(place * STRIPE, STRIPE), STRIPE)
            for kind, (source, there, send, recv) in enumerate(
                ((k_ref, kg, k_send, k_recv), (v_ref, vg, v_send, v_recv))
            ):
                push(
                    source.at[pl.ds(row, STRIPE), pl.ds(column, HD)],
                    there.at[target, pl.ds(0, HD)],
                    (2 * chip + kind, head), me, send.at[chip], recv,
                )
            return carry

        lax.fori_loop(0, CHIPS, send_keys, 0)

    def project(rows):
        return dot(rows, w_ref[...], CONTRACT_LAST).astype(BF16)

    part_row = lax.broadcasted_iota(jnp.int32, (SIDE, 64), 0)
    norm = n_ref[...].astype(F32) * (1.0 / SCALE)
    high = norm.astype(BF16).astype(F32)
    middle = (norm - high).astype(BF16).astype(F32)
    low = norm - high - middle
    for chunk in range(8):
        for h in range(2):
            cut = (slice(h, h + 1), slice(chunk * 64, (chunk + 1) * 64))
            rows = jnp.where(part_row == 0, high[cut], 0.0)
            rows = jnp.where(part_row == 1, middle[cut], rows)
            rows = jnp.where(part_row == 2, low[cut], rows)
            norms[chunk, h, :, 0:64] = rows

    def finish(chunk):
        rows = pl.ds(multiple(chunk * 64, 64), 64)
        for h in range(2):
            product = dl[chunk, h, 0:64, :].astype(F32) * o_ref[rows, h * HD:(h + 1) * HD].astype(F32)
            delta = jnp.sum(product.T, axis=0, keepdims=True).astype(BF16).astype(F32)
            extra = jnp.where(part_row == 3, delta, norms[chunk, h, :, 0:64])
            dl[chunk, h, 64:80, :] = jnp.concatenate(
                [extra, jnp.zeros((SIDE, 64), F32)], axis=1
            ).astype(BF16)

        def send(step, carry):
            index = lax.rem(me + step, 8)
            push(
                dl.at[chunk, index % 2],
                dg.at[own_slot, chunk, own_piece],
                (task_of(index), head), me, d_send.at[index], d_recv.at[chunk],
            )
            return carry

        lax.fori_loop(0, 8, send, 0)

    for number in range(2):
        fetches[number].wait()
    for number in range(2, 5):
        fetches[number].start()
    grad = project(g_ref[...])
    for h in range(2):
        dl[head, h, 0:64, :] = grad[:, h * HD:(h + 1) * HD]
    finish(head)

    kg[:, HD:] = pick(TASK_K, 0, 2)
    vg[:, HD:] = pick(TASK_K, 3, 3)
    dk_sum[...] = jnp.zeros_like(dk_sum)
    dv_sum[...] = jnp.zeros_like(dv_sum)
    in_group = lax.broadcasted_iota(jnp.int32, (32, HD), 0)

    def coarse_of(slot):
        return group + slot * (7 - 2 * group)

    def number_rows(index, carry):
        slot, chunk, half, pair = index // 32, index // 4 % 8, index // 2 % 2, index % 2
        pair = coarse_of(slot) * 32 + half * 16 + chunk * 2 + pair
        block = 2 * pair + jnp.where(in_group >= sizes[2 * pair], 1, 0)
        row = half * 64 + index % 2 * 32
        row_block[slot, chunk, pl.ds(multiple(row, 32), 32), :] = block
        row_block[slot, chunk, pl.ds(multiple(128 + row, 32), 32), :] = block + 1
        return carry

    lax.fori_loop(0, 64, number_rows, 0)
    row_lane = lax.broadcasted_iota(jnp.int32, (1, HD), 1)

    def number_keys(index, carry):
        blocks = []
        for half in range(2):
            pair = (index * 1024 + half * ROWS + x * STRIPE) // 32
            part = row_lane // 32
            size = jnp.where(
                part < 2,
                jnp.where(part == 0, sizes[2 * pair], sizes[2 * pair + 2]),
                jnp.where(part == 2, sizes[2 * pair + 4], sizes[2 * pair + 6]),
            )
            blocks.append(2 * (pair + part) + jnp.where(row_lane % 32 >= size, 1, 0))
        key_block[index] = jnp.concatenate(blocks, axis=1)
        return carry

    lax.fori_loop(0, 8, number_keys, 0)

    def query_owner(index):
        slot, kind, half = index // 4, index // 2 % 2, index % 2
        return kind * SHARDS + 2 * coarse_of(slot) + half

    def relay(there, recv):
        half = there.at[:, pl.ds(0, HD)]
        return pltpu.make_async_remote_copy(
            src_ref=half, dst_ref=half, send_sem=relay_send, recv_sem=recv,
            device_id=(sibling, head), device_id_type=MESH,
        )

    def attend(turn, carry):
        chunk = lax.rem(head + 8 + (turn + 1) // 2 * (1 - 2 * (turn % 2)), 8)

        @pl.when(turn == 0)
        def _():
            wait_bytes(qg, q_recv)
            for kind, (there, recv) in enumerate(((kg, k_recv), (vg, v_recv))):
                @pl.when(core == kind)
                def _():
                    wait_bytes(there.at[:, pl.ds(0, HD)], recv)
                    relay(there, recv).start()
            for kind, (there, recv) in enumerate(((vg, v_recv), (kg, k_recv))):
                @pl.when(core == kind)
                def _():
                    wait_bytes(there.at[:, pl.ds(0, HD)], recv)

        wait_bytes(dg.at[:, chunk], d_recv.at[chunk])
        dq_sum[...] = jnp.zeros_like(dq_sum)
        for slot in range(2):
            extras[slot] = side([dg[slot, chunk, piece, 64:80, :] for piece in range(4)])
            turned[slot, 0] = qg[slot, chunk].T
            turned[slot, 1] = dg[slot, chunk, :, 0:64, :].reshape(256, HD).T
        later = None
        for number, wide in ((0, 1), (1, 1), (2, 1), (3, 1), (4, 4), (8, 1)):
            slot = 1 if number >= 4 else (number - group + 3) // 4
            pair = number - slot * (group + 1)
            keys = pl.ds(multiple(pair * 256, 256), wide * 256)
            mask = None
            if number < 4 or number == 8:
                own = row_block[slot, chunk]
                mask = jnp.concatenate([own, own], axis=1) > key_block[pair]
            grads = dg[slot, chunk, :, 0:64, :].reshape(256, HD)
            dq, dk, dv = tile(
                qg[slot, chunk], grads, turned[slot, 0], turned[slot, 1], extras[slot],
                kg[keys, :], vg[keys, :], mask,
            )
            for step in range(wide):
                dk_sum[pair + step] += dk[:, step * 256:(step + 1) * 256]
                dv_sum[pair + step] += dv[:, step * 256:(step + 1) * 256]
            if number < 4:
                dq_sum[slot] += dq
            else:
                later = dq if later is None else later + dq
        first = (dq_sum[0] * SCALE).astype(BF16)
        second = ((dq_sum[1] + later) * SCALE).astype(BF16)
        for index in range(8):
            part = (first, second)[index // 4]
            dq_part[chunk, index] = part[index % 4 * 64:(index % 4 + 1) * 64]

        def send(step, inner):
            index = lax.rem(me + step, 8)
            push(
                dq_part.at[chunk, index],
                rq.at[x, chunk, :, pl.ds(multiple(which * HD, HD), HD)],
                (query_owner(index), head), me, dq_send.at[index], dq_recv,
            )
            return inner

        lax.fori_loop(0, 8, send, 0)
        return carry

    def attended(step):
        return step // 4 * (2 * step - 7) + step // 7

    def step(index, carry):
        for sub in range(2):
            for direction in range(2):
                source = landed.at[index, direction]
                ring(direction, index, sub, source).wait_recv()

                @pl.when(index < 5)
                def _():
                    ring(direction, lax.rem(index + 2, 7), sub, source).start()

        away = index // 2 + 1
        chunks = (lax.rem(head + 8 - away, 8), lax.rem(head + away, 8))
        units = (index % 2, 1 - index % 2)
        grad = project(landed[index].reshape(2 * UNIT, 4096))
        for direction in range(2):
            rows = pl.ds(multiple(units[direction] * UNIT, UNIT), UNIT)
            for h in range(2):
                dl[chunks[direction], h, rows, :] = grad[
                    direction * UNIT:(direction + 1) * UNIT, h * HD:(h + 1) * HD
                ]

        @pl.when(index % 2 == 1)
        def _():
            finish(chunks[0])

        @pl.when((index % 2 == 1) | (index == 6))
        def _():
            finish(chunks[1])

        lax.fori_loop(attended(index), attended(index + 1), attend, 0)
        return carry

    lax.fori_loop(0, 7, step, 0)

    def across(index):
        return pltpu.make_async_remote_copy(
            src_ref=to_sibling.at[index], dst_ref=from_sibling.at[index],
            send_sem=sibling_send.at[index], recv_sem=sibling_recv.at[index],
            device_id=(sibling, head), device_id_type=MESH,
        )

    def narrow(step, carry):
        index = lax.rem(me // 2 + step, 8)
        there = pl.ds(multiple((1 - core) * STRIPE, STRIPE), STRIPE)
        to_sibling[index, 0] = (dk_sum[index, :, there] * SCALE).T.astype(BF16)
        to_sibling[index, 1] = dv_sum[index, :, there].T.astype(BF16)
        across(index).start()
        return carry

    def pass_on(step, carry):
        index = lax.rem(me // 2 + step, 8)
        here = pl.ds(multiple(core * STRIPE, STRIPE), STRIPE)
        across(index).wait_recv()
        key_part[index, 0] = (
            (dk_sum[index, :, here] * SCALE).T + from_sibling[index, 0].astype(F32)
        ).astype(BF16)
        key_part[index, 1] = (
            dv_sum[index, :, here].T + from_sibling[index, 1].astype(F32)
        ).astype(BF16)
        push(
            key_part.at[index],
            rk.at[y % 2, :, pl.ds(multiple(x * STRIPE, STRIPE), STRIPE), pl.ds(multiple(which * HD, HD), HD)],
            (SHARDS + 2 * index + core, head), me, part_send.at[index], part_recv,
        )
        return carry

    def both(step, carry):
        narrow(step + 2, carry)
        return pass_on(step, carry)

    lax.fori_loop(0, 2, narrow, 0)
    lax.fori_loop(0, 6, both, 0)
    lax.fori_loop(6, 8, pass_on, 0)

    for number in range(2, 5):
        fetches[number].wait()

    @pl.when(me < SHARDS)
    def _():
        def number_own(index, carry):
            pair = place * 16 + index
            own_block[pl.ds(multiple(index * 32, 32), 32), :] = 2 * pair + jnp.where(
                in_group >= sizes[2 * pair], 1, 0
            )
            return carry

        lax.fori_loop(0, 16, number_own, 0)
        for part in range(4):
            rows = slice(part * STRIPE, (part + 1) * STRIPE)
            block = own_block[rows, :].astype(F32)
            mask = block == block.T
            for h in range(2):
                columns = slice(h * HD, (h + 1) * HD)
                own_q = q_own[2 * part:2 * part + 2, :, columns].reshape(STRIPE, HD)
                own_d = dl[2 * part:2 * part + 2, h, 0:64, :].reshape(STRIPE, HD)
                dq, dk, dv = tile(
                    own_q, own_d, own_q.T, own_d.T,
                    side([dl[2 * part + number, h, 64:80, :] for number in range(2)]),
                    jnp.concatenate([k_own[rows, columns], pick(STRIPE, 0, 2)], axis=1),
                    jnp.concatenate([v_own[rows, columns], pick(STRIPE, 3, 3)], axis=1),
                    mask,
                )
                dq_own[rows, columns] = dq * SCALE
                dk_out[rows, columns] = (dk * SCALE).T.astype(BF16)
                dv_out[rows, columns] = dv.T.astype(BF16)

    for index in range(7):
        for direction in range(2):
            for sub in range(2):
                ring(direction, index, sub, landed.at[index, direction]).wait_send()
    relay(kg, k_recv).wait_send()

    def settle(index, carry):
        @pl.when(task_of(index) != me)
        def _():
            wait_bytes(q_ref.at[:, :, pl.ds(0, HD)], q_send.at[index])
            wait_bytes(dl.at[:, 0], d_send.at[index])
        return carry

    lax.fori_loop(0, 8, settle, 0)

    @pl.when(clean)
    def _():
        def settle_keys(chip, carry):
            for kind, (source, send) in enumerate(((k_ref, k_send), (v_ref, v_send))):
                @pl.when(2 * chip + kind != me)
                def _():
                    wait_bytes(source.at[pl.ds(0, STRIPE), pl.ds(0, HD)], send.at[chip])
            return carry

        lax.fori_loop(0, CHIPS, settle_keys, 0)

    wait_bytes(rq, dq_recv)

    def summed_queries():
        parts = [rq[stripe].reshape(ROWS, 256).astype(F32) for stripe in range(4)]
        return (parts[0] + parts[1]) + (parts[2] + parts[3])

    @pl.when(me < SHARDS)
    def _():
        dq_out[...] = (summed_queries() + dq_own[...]).astype(BF16)

    @pl.when(clean)
    def _():
        dq_out[...] = summed_queries().astype(BF16)
        wait_bytes(rk, part_recv)
        dk_out[...] = (rk[0, 0].astype(F32) + rk[1, 0].astype(F32)).astype(BF16)
        dv_out[...] = (rk[0, 1].astype(F32) + rk[1, 1].astype(F32)).astype(BF16)

    def settle_last(index, carry):
        across(index).wait_send()

        @pl.when(query_owner(index) != me)
        def _():
            wait_bytes(dq_part.at[:, index], dq_send.at[index])

        @pl.when(SHARDS + 2 * index + core != me)
        def _():
            wait_bytes(key_part.at[index], part_send.at[index])
        return carry

    lax.fori_loop(0, 8, settle_last, 0)


ANY = pl.BlockSpec(memory_space=pl.ANY)
VMEM = pl.BlockSpec(memory_space=pltpu.VMEM)
SMEM = pl.BlockSpec(memory_space=pltpu.SMEM)
DMA = pltpu.SemaphoreType.DMA
LIMIT = 56 * 1024 * 1024


def hand_on_kernel(*refs):
    for source, target in zip(refs[:3], refs[3:]):
        target[...] = source[...]


def hand_on(results):
    return pl.pallas_call(
        hand_on_kernel,
        name="hand_on",
        out_shape=(jax.ShapeDtypeStruct((ROWS, 256), BF16),) * 3,
        in_specs=[VMEM] * 3,
        out_specs=(VMEM,) * 3,
        compiler_params=pltpu.CompilerParams(vmem_limit_bytes=LIMIT),
    )(*results)


def shards(queries, keys, values, attn_out, out_grad, out_weight, log_norm, block_sizes):
    results = pl.pallas_call(
        layer_kernel,
        name="layer",
        out_shape=(jax.ShapeDtypeStruct((ROWS, 256), BF16),) * 3,
        in_specs=[SMEM] + [ANY] * 5 + [VMEM] * 2,
        out_specs=(VMEM,) * 3,
        scratch_shapes=[
            pltpu.VMEM((64, 4096), BF16),
            pltpu.VMEM((256, 4096), BF16),
            pltpu.VMEM((8, 64, 256), BF16),
            pltpu.VMEM((ROWS, 256), BF16),
            pltpu.VMEM((ROWS, 256), BF16),
            pltpu.VMEM((7, 2, UNIT, 4096), BF16),
            pltpu.VMEM((2, 8, 256, HD), BF16),
            pltpu.VMEM((2, 8, 4, 64 + SIDE, HD), BF16),
            pltpu.VMEM((TASK_K, 256), BF16),
            pltpu.VMEM((TASK_K, 256), BF16),
            pltpu.VMEM((8, 2, 64 + SIDE, HD), BF16),
            pltpu.VMEM((8, 2, SIDE, HD), F32),
            pltpu.VMEM((2, 256, HD), BF16),
            pltpu.VMEM((2, 2, HD, 256), BF16),
            pltpu.VMEM((2, 256, HD), F32),
            pltpu.VMEM((8, HD, 256), F32),
            pltpu.VMEM((8, HD, 256), F32),
            pltpu.VMEM((2, 8, 256, HD), jnp.int32),
            pltpu.VMEM((8, 1, 256), jnp.int32),
            pltpu.VMEM((ROWS, HD), jnp.int32),
            pltpu.VMEM((ROWS, 256), F32),
            pltpu.VMEM((8, 8, 64, HD), BF16),
            pltpu.VMEM((8, 2, STRIPE, HD), BF16),
            pltpu.VMEM((8, 2, STRIPE, HD), BF16),
            pltpu.VMEM((8, 2, STRIPE, HD), BF16),
            pltpu.VMEM((4, 8, 64, 256), BF16),
            pltpu.VMEM((2, 2, ROWS, 256), BF16),
            DMA((2, 7, 2)), DMA((2, 7, 2)), DMA((8,)), DMA((CHIPS,)), DMA((CHIPS,)), DMA((8,)),
            DMA, DMA, DMA, DMA((8,)),
            DMA((8,)), DMA, DMA((8,)), DMA((8,)), DMA((8,)), DMA, DMA, DMA((5,)),
        ],
        compiler_params=pltpu.CompilerParams(
            collective_id=0, has_side_effects=True, vmem_limit_bytes=LIMIT
        ),
    )(
        block_sizes, queries.reshape(8, 64, 256), keys, values, out_grad, out_weight, attn_out,
        log_norm.T,
    )
    return hand_on(results)


def solution(mesh):
    in_specs = (
        P("seq", "head"),
        P("seq", "head"),
        P("seq", "head"),
        P("seq", "head"),
        P(("seq", "head"), None),
        P("head", None),
        P("seq", "head"),
        P(),
    )
    out_specs = (P("seq", "head"), P("seq", "head"), P("seq", "head"))
    return jax.shard_map(shards, mesh=mesh, in_specs=in_specs, out_specs=out_specs, check_vma=False)
```
